32 devices in a mesh: vocab: 8 (over z, x), rows: 4 (over y, core).
Axes of the slice: x: 2, y: 2, z: 4, core: 2. Of those that a mesh axis runs over, the one named last changes fastest.
Arguments:
- hidden: bfloat16 [1024, 4608], P('rows'), may hold values from -6 to 6
- norm_gain: bfloat16 [4608], replicated, may hold values from 0.5 to 1.5
- embed_table: bfloat16 [16384, 4608], P('vocab', 'rows'), may hold values from -1 to 1
- tokens: int32 [1024], P('rows'), may hold values from 0 to 16383
- parents: int32 [1024], P('rows'), may hold values from 0 to 7
- prev_scores: float32 [1024], P('rows'), may hold values from -30 to -1
- lengths: int32 [1024], P('rows'), may hold values from 1 to 128
Outputs:
- log_probs: float32 [1024, 16384], P('rows', 'vocab')
- chosen_lp: float32 [1024], P('rows')
- normalized: float32 [1024], P('rows')
- next_embed: bfloat16 [1024, 4608], P('rows')
The draws below stay inside these ranges and needn't reach their ends.
All inputs are finite; a program needn't handle non-finite values.
Results may differ from the reference program's by a relative error of at most 0.0045.
Values may be sent and summed in bfloat16 or wider, within the bound.
A program may use at most 128 MiB of HBM per device.

```python
import math
import jax
import jax.numpy as jnp
from jax import lax

D = 4608
BEAMS = 8
ROWS = 1024
VOCAB = 16384


def draw_embed_table(key, part):
    key = jax.random.fold_in(key, 11)
    key_entries, key_scales = jax.random.split(key, 2)
    ramp = 0.85 + 0.3 * jnp.arange(VOCAB, dtype=jnp.float32) / VOCAB
    row_scale = jnp.exp(jax.random.uniform(key_scales, (VOCAB,), jnp.float32, math.log(0.5), math.log(2.5)))
    entries = jnp.clip(jax.random.normal(key_entries, (VOCAB, D), jnp.float32), -6.0, 6.0)
    factor = ramp * row_scale * (3.0 / math.sqrt(D))
    return jnp.clip(entries * factor[:, None], -1.0, 1.0).astype(jnp.bfloat16)


def touch_ends(result, key, low, top_value):
    longest = result.shape.index(max(result.shape))
    spots = []
    for shift in (0, 1):
        where = [jax.random.randint(jax.random.fold_in(key, axis), (), 0, length) for axis, length in enumerate(result.shape)]
        where[longest] = (where[longest] + shift) % result.shape[longest]
        spots.append(tuple(where))
    return result.at[spots[0]].set(low).at[spots[1]].set(top_value)


def shard_levels(own_key, extent, cuts, smallest, high):
    factor_of, own = 1.0, jax.random.fold_in(own_key, 6)
    for dim, shards_of in cuts:
        draws = jnp.exp(jax.random.uniform(jax.random.fold_in(own, dim), (shards_of,), jnp.float32, smallest / len(cuts), high / len(cuts)))
        factor_of = factor_of * jnp.repeat(draws, extent[dim] // shards_of).reshape([-1 if axis == dim else 1 for axis in range(len(extent))])
    return factor_of


def bell_draw(own_key, dims, deviation, most, cuts=(), kind=jnp.bfloat16):
    loudness = shard_levels(own_key, dims, cuts, -0.22, 0.18) if cuts else 1.0
    result = jax.random.normal(own_key, dims, jnp.float32) * deviation * loudness
    return jnp.minimum(jnp.maximum(result, -most), most).astype(kind)


def setup_inputs(seed: int = 0) -> dict:
    arg_keys = jax.random.split(jax.random.key(seed), 8)
    return {
        "hidden": bell_draw(arg_keys[0], (ROWS, D), 1.0, 6.0, ((0, 4),)),
        "norm_gain": jnp.clip(1.0 + 0.1 * jax.random.normal(arg_keys[1], (D,), jnp.float32), 0.5, 1.5).astype(jnp.bfloat16),
        "embed_table": draw_embed_table(jax.random.fold_in(arg_keys[7], 71), 0),
        "tokens": touch_ends(jax.random.randint(arg_keys[3], (ROWS,), 0, VOCAB), jax.random.fold_in(arg_keys[3], 1), 0, VOCAB - 1).astype(jnp.int32),
        "parents": touch_ends(jax.random.randint(arg_keys[4], (ROWS,), 0, BEAMS), jax.random.fold_in(arg_keys[4], 1), 0, BEAMS - 1).astype(jnp.int32),
        "prev_scores": jnp.clip(-30.0 + 29.0 * jax.random.uniform(arg_keys[5], (ROWS,), jnp.float32) ** shard_levels(arg_keys[5], (ROWS,), ((0, 4),), -0.2, 0.2), -30.0, -1.0),
        "lengths": touch_ends(jax.random.randint(arg_keys[6], (ROWS,), 1, 129), jax.random.fold_in(arg_keys[6], 1), 1, 128).astype(jnp.int32),
    }


soft_cap = 30.0
length_power = 0.6
norm_eps = 1e-06

def reference(hidden, norm_gain, embed_table, tokens, parents, prev_scores, lengths):
    states = hidden.astype(jnp.float32)
    meansq = lax.optimization_barrier(jnp.mean(states * states, axis=-1, keepdims=True))
    normed = (states * lax.rsqrt(meansq + norm_eps) * norm_gain.astype(jnp.float32)).astype(jnp.bfloat16)
    logits = lax.dot_general(normed, embed_table, (((1,), (1,)), ((), ())), preferred_element_type=jnp.float32)
    capped = soft_cap * jnp.tanh(logits / soft_cap)
    lse = jnp.log(lax.optimization_barrier(jnp.sum(jnp.exp(capped), axis=1)))
    log_probs = capped - lse[:, None]
    parent_rows = jnp.arange(ROWS, dtype=jnp.int32) // BEAMS * BEAMS + parents
    chosen_lp = capped[parent_rows, tokens] - lse[parent_rows]
    penalty = jnp.power((5.0 + lengths.astype(jnp.float32)) / 6.0, length_power)
    normalized = (prev_scores[parent_rows] + chosen_lp) / penalty
    next_embed = (embed_table[tokens].astype(jnp.float32) * math.sqrt(D)).astype(jnp.bfloat16)
    return (log_probs, chosen_lp, normalized, next_embed)
```

```python
import math

import jax
import jax.numpy as jnp
from jax import lax
from jax.sharding import PartitionSpec as P

BEAMS = 8


soft_cap = 30.0
length_power = 0.6
norm_eps = 1e-06


def by_parent(values, parents):
    groups = values.reshape(-1, 1, BEAMS)
    hit = parents.reshape(-1, BEAMS, 1) == jnp.arange(BEAMS, dtype=jnp.int32)
    return jnp.sum(jnp.where(hit, groups, 0.0), axis=2).reshape(-1)


def local(shards, hidden, norm_gain, embed_table, tokens, parents, prev_scores, lengths):
    shard_index = lax.axis_index("vocab")
    voc_rows = embed_table.shape[0]
    row_count, width = hidden.shape
    scale = math.sqrt(width)

    all_tokens = lax.all_gather(tokens, "rows", axis=0, tiled=False)
    groups = all_tokens.shape[0]
    piece = row_count // shards
    order = all_tokens.reshape(groups, shards, piece).transpose(1, 0, 2).reshape(-1)
    all_col = order - shard_index * voc_rows
    all_inside = (all_col >= 0) & (all_col < voc_rows)
    picked = jnp.take(embed_table, jnp.clip(all_col, 0, voc_rows - 1), axis=0)
    picked = jnp.where(all_inside[:, None], picked, jnp.zeros((), jnp.bfloat16))
    summed = lax.psum_scatter(picked, "vocab", scatter_dimension=0, tiled=True)

    states = hidden.astype(jnp.float32)
    meansq = jnp.mean(states * states, axis=-1, keepdims=True)
    normed = (states * lax.rsqrt(meansq + norm_eps) * norm_gain.astype(jnp.float32)).astype(
        jnp.bfloat16
    )
    feature_cols = lax.all_to_all(normed, "rows", split_axis=1, concat_axis=0, tiled=True)
    logits = lax.psum_scatter(
        lax.dot_general(
            feature_cols, embed_table, (((1,), (1,)), ((), ())), preferred_element_type=jnp.float32
        ).astype(jnp.bfloat16),
        "rows",
        scatter_dimension=0,
        tiled=True,
    ).astype(jnp.float32)

    quarter = lax.all_to_all(summed, "rows", split_axis=0, concat_axis=1, tiled=True)
    quarter = (quarter.astype(jnp.float32) * scale).astype(jnp.bfloat16)
    next_embed = lax.all_gather(quarter, "vocab", axis=0, tiled=True)

    local_col = tokens - shard_index * voc_rows
    inside = (local_col >= 0) & (local_col < voc_rows)
    clipped_col = jnp.clip(local_col, 0, voc_rows - 1)
    capped = soft_cap * jnp.tanh(logits / soft_cap)
    sum_exp = jnp.sum(jnp.exp(capped), axis=1)
    parent_rows = jnp.arange(row_count, dtype=jnp.int32) // BEAMS * BEAMS + parents
    chosen_local = jnp.where(inside, capped[parent_rows, clipped_col], 0.0)
    total_exp, chosen_logit = lax.psum((sum_exp, chosen_local), "vocab")
    lse = jnp.log(total_exp)
    log_probs = capped - lse[:, None]
    chosen_lp = chosen_logit - by_parent(lse, parents)
    penalty = jnp.power((5.0 + lengths.astype(jnp.float32)) / 6.0, length_power)
    normalized = (by_parent(prev_scores, parents) + chosen_lp) / penalty
    return (log_probs, chosen_lp, normalized, next_embed)


def solution(mesh):
    placed = (P("rows", None), P(), P("vocab", "rows"), P("rows"), P("rows"), P("rows"), P("rows"))
    shards = mesh.shape["vocab"]
    return jax.shard_map(
        lambda *args: local(shards, *args),
        mesh=mesh,
        in_specs=placed,
        out_specs=(P("rows", "vocab"), P("rows"), P("rows"), P("rows", None)),
        check_vma=False,
    )
```

```python
import functools
import math

import jax
import jax.numpy as jnp
from jax import lax
from jax.experimental import pallas as pl
from jax.experimental.pallas import tpu as pltpu
from jax.sharding import PartitionSpec as P

BEAMS = 8


soft_cap = 30.0
length_power = 0.6
norm_eps = 1e-06


def by_parent(values, parents):
    groups = values.reshape(-1, 1, BEAMS)
    hit = parents.reshape(-1, BEAMS, 1) == jnp.arange(BEAMS, dtype=jnp.int32)
    return jnp.sum(jnp.where(hit, groups, 0.0), axis=2).reshape(-1)


def plain(shards, hidden, norm_gain, embed_table, tokens, parents, prev_scores, lengths):
    shard_index = lax.axis_index("vocab")
    voc_rows = embed_table.shape[0]
    row_count, width = hidden.shape
    scale = math.sqrt(width)

    all_tokens = lax.all_gather(tokens, "rows", axis=0, tiled=False)
    groups = all_tokens.shape[0]
    piece = row_count // shards
    order = all_tokens.reshape(groups, shards, piece).transpose(1, 0, 2).reshape(-1)
    all_col = order - shard_index * voc_rows
    all_inside = (all_col >= 0) & (all_col < voc_rows)
    picked = jnp.take(embed_table, jnp.clip(all_col, 0, voc_rows - 1), axis=0)
    picked = jnp.where(all_inside[:, None], picked, jnp.zeros((), jnp.bfloat16))
    summed = lax.psum_scatter(picked, "vocab", scatter_dimension=0, tiled=True)

    states = hidden.astype(jnp.float32)
    meansq = jnp.mean(states * states, axis=-1, keepdims=True)
    normed = (states * lax.rsqrt(meansq + norm_eps) * norm_gain.astype(jnp.float32)).astype(
        jnp.bfloat16
    )
    feature_cols = lax.all_to_all(normed, "rows", split_axis=1, concat_axis=0, tiled=True)
    logits = lax.psum_scatter(
        lax.dot_general(
            feature_cols, embed_table, (((1,), (1,)), ((), ())), preferred_element_type=jnp.float32
        ).astype(jnp.bfloat16),
        "rows",
        scatter_dimension=0,
        tiled=True,
    ).astype(jnp.float32)

    quarter = lax.all_to_all(summed, "rows", split_axis=0, concat_axis=1, tiled=True)
    quarter = (quarter.astype(jnp.float32) * scale).astype(jnp.bfloat16)
    next_embed = lax.all_gather(quarter, "vocab", axis=0, tiled=True)

    local_col = tokens - shard_index * voc_rows
    inside = (local_col >= 0) & (local_col < voc_rows)
    clipped_col = jnp.clip(local_col, 0, voc_rows - 1)
    capped = soft_cap * jnp.tanh(logits / soft_cap)
    sum_exp = jnp.sum(jnp.exp(capped), axis=1)
    parent_rows = jnp.arange(row_count, dtype=jnp.int32) // BEAMS * BEAMS + parents
    chosen_local = jnp.where(inside, capped[parent_rows, clipped_col], 0.0)
    total_exp, chosen_logit = lax.psum((sum_exp, chosen_local), "vocab")
    lse = jnp.log(total_exp)
    log_probs = capped - lse[:, None]
    chosen_lp = chosen_logit - by_parent(lse, parents)
    penalty = jnp.power((5.0 + lengths.astype(jnp.float32)) / 6.0, length_power)
    normalized = (by_parent(prev_scores, parents) + chosen_lp) / penalty
    return (log_probs, chosen_lp, normalized, next_embed)


LINE = 4
QUARTERS = 4
TILES = 4
DEPTH = 512


def kernel(
    hidden_ref, gain_ref, table_ref, aux_ref, cap_out, stat_out, emb_out,
    hid, table, nrm, far, aux_in, tok_t, tok_p, acc, picked, from_left, from_right, from_x,
    quarters, emb, own, part_near, part_far, part_y, got_near, got_far, got_y, cap,
    sum_e, sum_c, stat_in, load_sem, out_sem, send_sem, recv_sem,
):
    v, r = lax.axis_index("vocab"), lax.axis_index("rows")
    z, x, y, c = v // 2, v % 2, r // 2, r % 2
    shards = 2 * LINE
    other_x = z * 2 + (1 - x)
    sib = y * 2 + (1 - c)
    far_same = (1 - y) * 2 + c
    far_sib = (1 - y) * 2 + (1 - c)
    voc_rows, depth = table.shape
    rows = hid.shape[0]
    piece = rows // shards
    width = voc_rows // TILES

    sites = []

    class Site:
        def __init__(self, cond, src, dst, device):
            k = len(sites)
            sites.append(self)
            self.cond = cond
            self.copy = pltpu.make_async_remote_copy(
                src_ref=src, dst_ref=dst, send_sem=send_sem.at[k], recv_sem=recv_sem.at[k],
                device_id=device, device_id_type=pl.DeviceIdType.MESH,
            )

        def start(self):
            self.when(self.cond, self.copy.start)

        def sent(self):
            self.when(self.cond, self.copy.wait_send)

        def arrived(self):
            self.copy.wait_recv()

        @staticmethod
        def when(cond, action):
            if cond is None:
                action()
            else:
                pl.when(cond)(action)

    def both(*conds):
        return functools.reduce(jnp.logical_and, conds)

    load_hidden = pltpu.make_async_copy(hidden_ref, hid, load_sem.at[0])
    load_table = pltpu.make_async_copy(table_ref, table, load_sem.at[1])
    load_hidden.start()
    load_table.start()

    barrier = pltpu.get_barrier_semaphore()
    for step in range(1, QUARTERS):
        pl.semaphore_signal(barrier, inc=1, device_id=(v, (r + step) % QUARTERS),
                            device_id_type=pl.DeviceIdType.MESH)
    for step in range(1, shards):
        pl.semaphore_signal(barrier, inc=1, device_id=((v + step) % shards, r),
                            device_id_type=pl.DeviceIdType.MESH)
    pl.semaphore_wait(barrier, QUARTERS + shards - 2)

    aux_sites = [Site(None, aux_ref, aux_in.at[s], (v, (r + s) % QUARTERS)) for s in range(1, QUARTERS)]
    for site in aux_sites:
        site.start()

    load_hidden.wait()
    gain = gain_ref[...].astype(jnp.float32)

    def norm_step(i, _):
        at = pl.ds(pl.multiple_of(i * 16, 16), 16)
        states = hid[at, :].astype(jnp.float32)
        meansq = jnp.mean(states * states, axis=-1, keepdims=True)
        normed = (states * lax.rsqrt(meansq + norm_eps) * gain).astype(jnp.bfloat16)
        for q in range(QUARTERS):
            nrm[q, at, :] = normed[:, q * depth:(q + 1) * depth]
        return 0

    lax.fori_loop(0, rows // 16, norm_step, 0)
    hid_far_sib = Site(None, nrm.at[far_sib], far.at[0], (v, far_sib))
    hid_far_same = Site(None, nrm.at[far_same], far.at[1], (v, far_same))
    hid_sib = Site(None, nrm.at[sib], far.at[2], (v, sib))
    hid_sib.start()
    hid_far_sib.start()
    hid_far_same.start()

    def columns(block):
        return jnp.concatenate([block] * (128 // 8), axis=0).T

    tok_t[r] = columns(aux_ref[...])
    for s, site in enumerate(aux_sites, 1):
        site.arrived()
        tok_t[(r + QUARTERS - s) % QUARTERS] = columns(aux_in[s])
    for p in range(shards):
        for q in range(QUARTERS):
            tok_p[p // 2, p % 2, q] = tok_t[q, p * piece:(p + 1) * piece, :]
    load_table.wait()

    base = (v * voc_rows).astype(jnp.float32)
    group = QUARTERS * piece

    def lookup(za, xa, zb, xb):
        tok = jnp.concatenate(
            [tok_p[za, xa].reshape(group, 128), tok_p[zb, xb].reshape(group, 128)], axis=0
        )[:, :1] - base

        def step(k, _):
            entry = lax.broadcasted_iota(jnp.int32, (2 * group, DEPTH), 1) + k * DEPTH
            hot = jnp.where(entry.astype(jnp.float32) == tok, 1.0, 0.0).astype(jnp.bfloat16)
            at = pl.ds(pl.multiple_of(k * DEPTH, DEPTH), DEPTH)
            acc[...] += jnp.dot(hot, table[at, :], preferred_element_type=jnp.float32)
            return 0

        acc[...] = jnp.zeros_like(acc)
        lax.fori_loop(0, voc_rows // DEPTH, step, 0)
        for half, (zz, xx) in enumerate(((za, xa), (zb, xb))):
            block = acc[half * group:(half + 1) * group, :].astype(jnp.bfloat16)
            picked[zz, xx] = block.reshape(QUARTERS, piece, depth)

    even, odd = c == 0, c == 1
    right, left = (z + 1) * 2 + x, (z - 1) * 2 + x

    def line_sites(kind, view):
        to_right, to_left = {}, {}
        for j in range(LINE):
            if j > 0:
                to_right[j] = Site(both(kind, z < j), view(picked, j), view(from_left, j), (right, r))
            if j < LINE - 1:
                to_left[j] = Site(both(kind, z > j), view(picked, j), view(from_right, j), (left, r))
        return to_right, to_left

    even_right, even_left = line_sites(even, lambda ref, j: ref.at[j, x])
    odd_right, odd_left = line_sites(odd, lambda ref, j: ref.at[j])
    even_x = [Site(even, picked.at[j, 1 - x], from_x.at[j], (other_x, r)) for j in range(LINE)]
    odd_x = Site(odd, picked.at[z, 1 - x], from_x.at[0], (other_x, r))

    def add(dst, src):
        def one(i, _):
            dst[i] = dst[i] + src[i]
            return 0

        lax.fori_loop(0, QUARTERS, one, 0)

    def line_step(kind, sites_right, sites_left, s, view):
        j = LINE - 1 - s
        site = sites_right[j]

        def pass_right():
            site.arrived()
            for dst, got in view(j, from_left):
                add(dst, got)

        pl.when(both(kind, z > 0, z <= j))(pass_right)
        other = sites_left[s]

        def pass_left():
            other.arrived()
            for dst, got in view(s, from_right):
                add(dst, got)

        def send_right():
            pl.when(both(kind, z > 0))(site.start)

        def send_left():
            pl.when(both(kind, z < LINE - 1))(other.start)

        send_right()
        pl.when(both(kind, z < LINE - 1, z >= s))(pass_left)
        send_left()

    even_view = lambda j, ref: [(picked.at[j, x], ref.at[j, x])]
    odd_view = lambda j, ref: [(picked.at[j, xx], ref.at[j, xx]) for xx in range(2)]

    order = (LINE - 1, 0, LINE - 2, 1)
    for i, o in enumerate(order):
        first = 2 * (i % 2)
        xe = (1 - x) if i < 2 else x
        lookup((1 - c) * first + c * o, (1 - c) * xe, (1 - c) * (first + 1) + c * o, (1 - c) * xe + c)
        if i < 2:
            even_x[first].start()
            even_x[first + 1].start()
        if o > 0:
            pl.when(z == 0)(odd_right[o].start)
        if o < LINE - 1:
            pl.when(z == LINE - 1)(odd_left[o].start)

    def product(block, t):
        at = pl.ds(pl.multiple_of(t * width, width), width)
        return lax.dot_general(block, table[at, :], (((1,), (1,)), ((), ())),
                               preferred_element_type=jnp.float32)

    near_sites = [Site(None, part_near.at[t], got_near.at[t], (v, sib)) for t in range(TILES)]
    far_sites = [Site(None, part_far.at[t], got_far.at[t], (v, sib)) for t in range(TILES)]
    y_sites = [Site(None, part_y.at[t], got_y.at[t], (v, far_same)) for t in range(TILES)]

    hid_sib.arrived()
    for t in range(TILES):
        part_near[t] = product(far[2], t).astype(jnp.bfloat16)
        near_sites[t].start()

    def own_step(t, _):
        own[t] = product(nrm[r], t)
        return 0

    lax.fori_loop(0, TILES, own_step, 0)

    for s in range(LINE - 1):
        line_step(odd, odd_right, odd_left, s, odd_view)

    def odd_last():
        odd_x.copy.start()

    pl.when(odd)(odd_last)
    for j in range(LINE):
        def take(j=j):
            even_x[j].arrived()
            add(picked.at[j, x], from_x.at[j])

        pl.when(even)(take)
    for j in range(1, LINE):
        pl.when(both(even, z == 0))(even_right[LINE - j].copy.start)
        pl.when(both(even, z == LINE - 1))(even_left[j - 1].copy.start)
    line_step(even, even_right, even_left, 0, even_view)

    hid_far_sib.arrived()
    for t in range(TILES):
        part_far[t] = product(far[0], t).astype(jnp.bfloat16)
        far_sites[t].start()
    hid_far_same.arrived()
    for t in range(TILES):
        mine = product(far[1], t)
        far_sites[t].arrived()
        part_y[t] = (mine + got_far[t].astype(jnp.float32)).astype(jnp.bfloat16)
        y_sites[t].start()

    for s in range(1, LINE - 1):
        line_step(even, even_right, even_left, s, even_view)

    def odd_take():
        odd_x.arrived()
        add(picked.at[z, x], from_x.at[0])

    pl.when(odd)(odd_take)

    quarter_sites = [
        Site(None, picked.at[z, x, (r + s) % QUARTERS], quarters.at[s], (v, (r + s) % QUARTERS))
        for s in range(1, QUARTERS)
    ]
    for site in quarter_sites:
        site.start()
    whole = emb.at[z, x]

    def place(q, block):
        for k in range(QUARTERS):
            @pl.when(q == k)
            def _(k=k):
                whole[:, k * depth:(k + 1) * depth] = block

    place(r, picked[z, x, r])
    for s, site in enumerate(quarter_sites, 1):
        site.arrived()
        place((r + QUARTERS - s) % QUARTERS, quarters[s])

    go_right, go_left, go_x = {}, {}, {}
    for j in range(LINE):
        for xx in range(2):
            mine = jnp.logical_or(odd, x == xx)
            src = emb.at[j, xx]
            go_right[j, xx] = Site(both(mine, z >= j, z < LINE - 1), src, src, (right, r))
            go_left[j, xx] = Site(both(mine, z <= j, z > 0), src, src, (left, r))
            go_x[j, xx] = Site(both(x == xx, jnp.logical_or(even, z == j)), src, src, (other_x, r))

    def each(j, cond, action):
        for xx in range(2):
            pl.when(both(cond, z == j, xx == x))(functools.partial(action, j, xx))

    for j in range(LINE):
        for xx in range(2):
            here = both(z == j, x == xx)
            for group_of in (go_right, go_left, go_x):
                site = group_of[j, xx]
                pl.when(both(here, site.cond))(site.copy.start)
    for j in range(LINE):
        for xx in range(2):
            there = both(odd, z == j, x == 1 - xx)

            def from_neighbour(j=j, xx=xx):
                go_x[j, xx].arrived()

            pl.when(there)(from_neighbour)
            for group_of in (go_right, go_left):
                site = group_of[j, xx]
                pl.when(both(there, site.cond))(site.copy.start)

    def gather_step(d):
        for j in range(LINE):
            for xx in range(2):
                mine = jnp.logical_or(odd, x == xx)
                if j + d < LINE:
                    at = both(mine, z == j + d)
                    pl.when(at)(go_right[j, xx].arrived)
                    pl.when(both(at, go_right[j, xx].cond))(go_right[j, xx].copy.start)
                    pl.when(both(at, go_x[j, xx].cond))(go_x[j, xx].copy.start)
                if j - d >= 0:
                    at = both(mine, z == j - d)
                    pl.when(at)(go_left[j, xx].arrived)
                    pl.when(both(at, go_left[j, xx].cond))(go_left[j, xx].copy.start)
                    pl.when(both(at, go_x[j, xx].cond))(go_x[j, xx].copy.start)

    gather_step(1)
    gather_step(2)

    sum_e[...] = jnp.zeros_like(sum_e)
    sum_c[...] = jnp.zeros_like(sum_c)
    some = 32
    out_copies = []
    for t in range(TILES):
        near_sites[t].arrived()
        y_sites[t].arrived()

        def cap_step(i, _, t=t):
            at = pl.ds(pl.multiple_of(i * some, some), some)
            logits = own[t, at, :] + got_near[t, at, :].astype(jnp.float32)
            logits = logits + got_y[t, at, :].astype(jnp.float32)
            capped = soft_cap * jnp.tanh(logits / soft_cap)
            cap[at, t * width:(t + 1) * width] = capped
            exps = jnp.exp(capped)
            about = tok_t[r, at, :]
            parent = about[:, 1:2].reshape(some // BEAMS, BEAMS, 1)
            beams = capped.reshape(some // BEAMS, BEAMS, width)
            chosen = jnp.zeros_like(beams)
            for b in range(BEAMS):
                chosen = jnp.where(parent == float(b), beams[:, b:b + 1, :], chosen)
            entry = lax.broadcasted_iota(jnp.int32, (some, width), 1) + t * width
            hit = entry.astype(jnp.float32) == about[:, 0:1] - base
            chosen = jnp.where(hit, chosen.reshape(some, width), 0.0)
            for k in range(0, width, 128):
                sum_e[at, :] += exps[:, k:k + 128]
                sum_c[at, :] += chosen[:, k:k + 128]
            return 0

        lax.fori_loop(0, rows // some, cap_step, 0)
        span = pl.ds(t * width, width)
        copy = pltpu.make_async_copy(cap.at[:, span], cap_out.at[:, span], out_sem.at[t])
        copy.start()
        out_copies.append(copy)
    lane = lax.broadcasted_iota(jnp.int32, (rows, 128), 1)
    total_e = jnp.sum(sum_e[...], axis=1, keepdims=True)
    total_c = jnp.sum(sum_c[...], axis=1, keepdims=True)
    stat = jnp.where(lane == 0, total_e, jnp.where(lane == 1, total_c, 0.0)).T[:8]
    stat_in[0] = stat
    stat_sites = [Site(None, stat_in.at[0], stat_in.at[s], ((v + s) % shards, r)) for s in range(1, shards)]
    for site in stat_sites:
        site.start()

    gather_step(3)
    for j in range(LINE):
        for xx in range(2):
            pl.when(both(even, x == 1 - xx))(go_x[j, xx].arrived)
    emb_copy = pltpu.make_async_copy(emb, emb_out, out_sem.at[TILES])
    emb_copy.start()
    for s, site in enumerate(stat_sites, 1):
        site.arrived()
        stat = stat + stat_in[s]
    stat_out[...] = stat
    for site in sites:
        site.sent()
    for copy in out_copies:
        copy.wait()
    emb_copy.wait()


def fused(hidden, norm_gain, embed_table, tokens, parents, prev_scores, lengths):
    shards = 2 * LINE
    voc_rows, depth = embed_table.shape
    rows, features = hidden.shape
    piece = rows // shards
    width = voc_rows // TILES
    aux = jnp.zeros((8, rows), jnp.float32).at[0].set(tokens.astype(jnp.float32))
    aux = aux.at[1].set(parents.astype(jnp.float32))
    half, full = jnp.bfloat16, jnp.float32
    anywhere, vmem = pl.BlockSpec(memory_space=pl.ANY), pl.BlockSpec(memory_space=pltpu.VMEM)
    tiles = pltpu.VMEM((TILES, rows, width), half)
    line = pltpu.VMEM((LINE, 2, QUARTERS, piece, depth), half)
    capped, stat, raw = pl.pallas_call(
        kernel,
        out_shape=(
            jax.ShapeDtypeStruct((rows, voc_rows), full),
            jax.ShapeDtypeStruct((8, rows), full),
            jax.ShapeDtypeStruct((LINE, 2, piece, features), half),
        ),
        in_specs=[anywhere, vmem, anywhere, vmem],
        out_specs=(anywhere, vmem, anywhere),
        scratch_shapes=[
            pltpu.VMEM((rows, features), half),
            pltpu.VMEM((voc_rows, depth), half),
            pltpu.VMEM((QUARTERS, rows, depth), half),
            pltpu.VMEM((3, rows, depth), half),
            pltpu.VMEM((QUARTERS, 8, rows), full),
            pltpu.VMEM((QUARTERS, rows, 128), full),
            pltpu.VMEM((LINE, 2, QUARTERS, piece, 128), full),
            pltpu.VMEM((2 * QUARTERS * piece, depth), full),
            line,
            line,
            line,
            pltpu.VMEM((LINE, QUARTERS, piece, depth), half),
            pltpu.VMEM((QUARTERS, piece, depth), half),
            pltpu.VMEM((LINE, 2, piece, features), half),
            pltpu.VMEM((TILES, rows, width), full),
            tiles, tiles, tiles, tiles, tiles, tiles,
            pltpu.VMEM((rows, voc_rows), full),
            pltpu.VMEM((rows, 128), full),
            pltpu.VMEM((rows, 128), full),
            pltpu.VMEM((shards, 8, rows), full),
            pltpu.SemaphoreType.DMA((2,)),
            pltpu.SemaphoreType.DMA((TILES + 1,)),
            pltpu.SemaphoreType.DMA((80,)),
            pltpu.SemaphoreType.DMA((80,)),
        ],
        compiler_params=pltpu.CompilerParams(
            collective_id=0, has_side_effects=True, vmem_limit_bytes=58 * 2**20
        ),
        cost_estimate=pl.CostEstimate(
            flops=8 * rows * QUARTERS // 2 * voc_rows * depth, bytes_accessed=12 * 2**20,
            transcendentals=2 * rows * voc_rows,
        ),
    )(hidden, norm_gain.reshape(1, features), embed_table, aux)
    lse = jnp.log(stat[0])
    log_probs = capped - lse[:, None]
    chosen_lp = stat[1] - by_parent(lse, parents)
    penalty = jnp.power((5.0 + lengths.astype(full)) / 6.0, length_power)
    normalized = (by_parent(prev_scores, parents) + chosen_lp) / penalty
    next_embed = (raw.reshape(rows, features).astype(full) * math.sqrt(features)).astype(half)
    return (log_probs, chosen_lp, normalized, next_embed)


def solution(mesh):
    placed = (P("rows", None), P(), P("vocab", "rows"), P("rows"), P("rows"), P("rows"), P("rows"))
    shards = mesh.shape["vocab"]
    fits = shards == 2 * LINE and mesh.shape["rows"] == QUARTERS
    return jax.shard_map(
        fused if fits else functools.partial(plain, shards),
        mesh=mesh,
        in_specs=placed,
        out_specs=(P("rows", "vocab"), P("rows"), P("rows"), P("rows", None)),
        check_vma=False,
    )
```

```python
import functools
import math

import jax
import jax.numpy as jnp
from jax import lax
from jax.experimental import pallas as pl
from jax.experimental.pallas import tpu as pltpu
from jax.sharding import PartitionSpec as P

BEAMS = 8


soft_cap = 30.0
length_power = 0.6
norm_eps = 1e-06


def by_parent(values, parents):
    groups = values.reshape(-1, 1, BEAMS)
    hit = parents.reshape(-1, BEAMS, 1) == jnp.arange(BEAMS, dtype=jnp.int32)
    return jnp.sum(jnp.where(hit, groups, 0.0), axis=2).reshape(-1)


def plain(shards, hidden, norm_gain, embed_table, tokens, parents, prev_scores, lengths):
    shard_index = lax.axis_index("vocab")
    voc_rows = embed_table.shape[0]
    row_count, width = hidden.shape
    scale = math.sqrt(width)

    all_tokens = lax.all_gather(tokens, "rows", axis=0, tiled=False)
    groups = all_tokens.shape[0]
    piece = row_count // shards
    order = all_tokens.reshape(groups, shards, piece).transpose(1, 0, 2).reshape(-1)
    all_col = order - shard_index * voc_rows
    all_inside = (all_col >= 0) & (all_col < voc_rows)
    picked = jnp.take(embed_table, jnp.clip(all_col, 0, voc_rows - 1), axis=0)
    picked = jnp.where(all_inside[:, None], picked, jnp.zeros((), jnp.bfloat16))
    summed = lax.psum_scatter(picked, "vocab", scatter_dimension=0, tiled=True)

    states = hidden.astype(jnp.float32)
    meansq = jnp.mean(states * states, axis=-1, keepdims=True)
    normed = (states * lax.rsqrt(meansq + norm_eps) * norm_gain.astype(jnp.float32)).astype(
        jnp.bfloat16
    )
    feature_cols = lax.all_to_all(normed, "rows", split_axis=1, concat_axis=0, tiled=True)
    logits = lax.psum_scatter(
        lax.dot_general(
            feature_cols, embed_table, (((1,), (1,)), ((), ())), preferred_element_type=jnp.float32
        ).astype(jnp.bfloat16),
        "rows",
        scatter_dimension=0,
        tiled=True,
    ).astype(jnp.float32)

    quarter = lax.all_to_all(summed, "rows", split_axis=0, concat_axis=1, tiled=True)
    quarter = (quarter.astype(jnp.float32) * scale).astype(jnp.bfloat16)
    next_embed = lax.all_gather(quarter, "vocab", axis=0, tiled=True)

    local_col = tokens - shard_index * voc_rows
    inside = (local_col >= 0) & (local_col < voc_rows)
    clipped_col = jnp.clip(local_col, 0, voc_rows - 1)
    capped = soft_cap * jnp.tanh(logits / soft_cap)
    sum_exp = jnp.sum(jnp.exp(capped), axis=1)
    parent_rows = jnp.arange(row_count, dtype=jnp.int32) // BEAMS * BEAMS + parents
    chosen_local = jnp.where(inside, capped[parent_rows, clipped_col], 0.0)
    total_exp, chosen_logit = lax.psum((sum_exp, chosen_local), "vocab")
    lse = jnp.log(total_exp)
    log_probs = capped - lse[:, None]
    chosen_lp = chosen_logit - by_parent(lse, parents)
    penalty = jnp.power((5.0 + lengths.astype(jnp.float32)) / 6.0, length_power)
    normalized = (by_parent(prev_scores, parents) + chosen_lp) / penalty
    return (log_probs, chosen_lp, normalized, next_embed)


LINE = 4
QUARTERS = 4
TILES = 4
DEPTH = 512


def kernel(
    hidden_ref, gain_ref, table_ref, aux_ref, cap_out, stat_out, emb_out,
    hid, table, nrm, far, aux_in, tok_t, tok_p, acc, picked, from_left, from_right, from_x,
    quarters, emb, own, part_near, part_far, part_y, got_near, got_far, got_y, cap,
    sum_e, sum_c, stat_in, load_sem, out_sem, send_sem, recv_sem,
):
    v, r = lax.axis_index("vocab"), lax.axis_index("rows")
    z, x, y, c = v // 2, v % 2, r // 2, r % 2
    shards = 2 * LINE
    other_x = z * 2 + (1 - x)
    sib = y * 2 + (1 - c)
    far_same = (1 - y) * 2 + c
    far_sib = (1 - y) * 2 + (1 - c)
    voc_rows, depth = table.shape
    rows = hid.shape[0]
    piece = rows // shards
    width = voc_rows // TILES

    sites = []

    class Site:
        def __init__(self, cond, src, dst, device):
            k = len(sites)
            sites.append(self)
            self.cond = cond
            self.copy = pltpu.make_async_remote_copy(
                src_ref=src, dst_ref=dst, send_sem=send_sem.at[k], recv_sem=recv_sem.at[k],
                device_id=device, device_id_type=pl.DeviceIdType.MESH,
            )

        def start(self):
            self.when(self.cond, self.copy.start)

        def sent(self):
            self.when(self.cond, self.copy.wait_send)

        def arrived(self):
            self.copy.wait_recv()

        @staticmethod
        def when(cond, action):
            if cond is None:
                action()
            else:
                pl.when(cond)(action)

    def both(*conds):
        return functools.reduce(jnp.logical_and, conds)

    load_hidden = pltpu.make_async_copy(hidden_ref, hid, load_sem.at[0])
    load_table = pltpu.make_async_copy(table_ref, table, load_sem.at[1])
    load_hidden.start()
    load_table.start()

    barrier = pltpu.get_barrier_semaphore()
    for step in range(1, QUARTERS):
        pl.semaphore_signal(barrier, inc=1, device_id=(v, (r + step) % QUARTERS),
                            device_id_type=pl.DeviceIdType.MESH)
    for step in range(1, shards):
        pl.semaphore_signal(barrier, inc=1, device_id=((v + step) % shards, r),
                            device_id_type=pl.DeviceIdType.MESH)
    pl.semaphore_wait(barrier, QUARTERS + shards - 2)

    aux_sites = [Site(None, aux_ref, aux_in.at[s], (v, (r + s) % QUARTERS)) for s in range(1, QUARTERS)]
    for site in aux_sites:
        site.start()

    load_hidden.wait()
    gain = gain_ref[...].astype(jnp.float32).reshape(1, QUARTERS * depth)

    def norm_step(i, _):
        at = pl.ds(pl.multiple_of(i * 16, 16), 16)
        states = hid[at, :].astype(jnp.float32)
        meansq = jnp.mean(states * states, axis=-1, keepdims=True)
        normed = (states * lax.rsqrt(meansq + norm_eps) * gain).astype(jnp.bfloat16)
        for q in range(QUARTERS):
            nrm[q, at, :] = normed[:, q * depth:(q + 1) * depth]
        return 0

    lax.fori_loop(0, rows // 16, norm_step, 0)
    hid_far_sib = Site(None, nrm.at[far_sib], far.at[0], (v, far_sib))
    hid_far_same = Site(None, nrm.at[far_same], far.at[1], (v, far_same))
    hid_sib = Site(None, nrm.at[sib], far.at[2], (v, sib))
    hid_sib.start()
    hid_far_sib.start()
    hid_far_same.start()

    def columns(block):
        return jnp.concatenate([block] * (128 // 8), axis=0).T

    tok_t[r] = columns(aux_ref[...])
    for s, site in enumerate(aux_sites, 1):
        site.arrived()
        tok_t[(r + QUARTERS - s) % QUARTERS] = columns(aux_in[s])
    for p in range(shards):
        for q in range(QUARTERS):
            tok_p[p // 2, p % 2, q] = tok_t[q, p * piece:(p + 1) * piece, :]
    load_table.wait()

    base = (v * voc_rows).astype(jnp.float32)
    group = QUARTERS * piece

    def lookup(za, xa, zb, xb):
        tok = jnp.concatenate(
            [tok_p[za, xa].reshape(group, 128), tok_p[zb, xb].reshape(group, 128)], axis=0
        )[:, :1] - base

        def step(k, _):
            entry = lax.broadcasted_iota(jnp.int32, (2 * group, DEPTH), 1) + k * DEPTH
            hot = jnp.where(entry.astype(jnp.float32) == tok, 1.0, 0.0).astype(jnp.bfloat16)
            at = pl.ds(pl.multiple_of(k * DEPTH, DEPTH), DEPTH)
            acc[...] += jnp.dot(hot, table[at, :], preferred_element_type=jnp.float32)
            return 0

        acc[...] = jnp.zeros_like(acc)
        lax.fori_loop(0, voc_rows // DEPTH, step, 0)
        for half, (zz, xx) in enumerate(((za, xa), (zb, xb))):
            block = acc[half * group:(half + 1) * group, :].astype(jnp.bfloat16)
            picked[zz, xx] = block.reshape(QUARTERS, piece, depth)

    even, odd = c == 0, c == 1
    right, left = (z + 1) * 2 + x, (z - 1) * 2 + x

    def line_sites(kind, view):
        to_right, to_left = {}, {}
        for j in range(LINE):
            if j > 0:
                to_right[j] = Site(both(kind, z < j), view(picked, j), view(from_left, j), (right, r))
            if j < LINE - 1:
                to_left[j] = Site(both(kind, z > j), view(picked, j), view(from_right, j), (left, r))
        return to_right, to_left

    even_right, even_left = line_sites(even, lambda ref, j: ref.at[j, x])
    odd_right, odd_left = line_sites(odd, lambda ref, j: ref.at[j])
    even_x = [Site(even, picked.at[j, 1 - x], from_x.at[j], (other_x, r)) for j in range(LINE)]
    odd_x = Site(odd, picked.at[z, 1 - x], from_x.at[0], (other_x, r))

    def add(dst, src):
        def one(i, _):
            dst[i] = dst[i] + src[i]
            return 0

        lax.fori_loop(0, QUARTERS, one, 0)

    def line_step(kind, sites_right, sites_left, s, view):
        j = LINE - 1 - s
        site = sites_right[j]

        def pass_right():
            site.arrived()
            for dst, got in view(j, from_left):
                add(dst, got)

        pl.when(both(kind, z > 0, z <= j))(pass_right)
        other = sites_left[s]

        def pass_left():
            other.arrived()
            for dst, got in view(s, from_right):
                add(dst, got)

        def send_right():
            pl.when(both(kind, z > 0))(site.start)

        def send_left():
            pl.when(both(kind, z < LINE - 1))(other.start)

        send_right()
        pl.when(both(kind, z < LINE - 1, z >= s))(pass_left)
        send_left()

    even_view = lambda j, ref: [(picked.at[j, x], ref.at[j, x])]
    odd_view = lambda j, ref: [(picked.at[j, xx], ref.at[j, xx]) for xx in range(2)]

    order = (LINE - 1, 0, LINE - 2, 1)
    for i, o in enumerate(order):
        ea, eb = order[2 * (i % 2)], order[2 * (i % 2) + 1]
        xe = (1 - x) if i < 2 else x
        lookup((1 - c) * ea + c * o, (1 - c) * xe, (1 - c) * eb + c * o, (1 - c) * xe + c)
        if i < 2:
            even_x[ea].start()
            even_x[eb].start()
        if o > 0:
            pl.when(z == 0)(odd_right[o].start)
        if o < LINE - 1:
            pl.when(z == LINE - 1)(odd_left[o].start)

    def product(block, t):
        at = pl.ds(pl.multiple_of(t * width, width), width)
        return lax.dot_general(block, table[at, :], (((1,), (1,)), ((), ())),
                               preferred_element_type=jnp.float32)

    near_sites = [Site(None, part_near.at[t], got_near.at[t], (v, sib)) for t in range(TILES)]
    far_sites = [Site(None, part_far.at[t], got_far.at[t], (v, sib)) for t in range(TILES)]
    y_sites = [Site(None, part_y.at[t], got_y.at[t], (v, far_same)) for t in range(TILES)]

    def near_products():
        hid_sib.arrived()
        for t in range(TILES):
            part_near[t] = product(far[2], t).astype(jnp.bfloat16)
            near_sites[t].start()

        def own_step(t, _):
            own[t] = product(nrm[r], t)
            return 0

        lax.fori_loop(0, TILES, own_step, 0)

    def even_ready(j):
        def take():
            even_x[j].arrived()
            add(picked.at[j, x], from_x.at[j])

        pl.when(even)(take)
        if j > 0:
            pl.when(both(even, z == 0))(even_right[j].copy.start)
        if j < LINE - 1:
            pl.when(both(even, z == LINE - 1))(even_left[j].copy.start)

    line_step(odd, odd_right, odd_left, 0, odd_view)
    even_ready(order[0])
    even_ready(order[1])
    line_step(odd, odd_right, odd_left, 1, odd_view)
    even_ready(order[2])
    even_ready(order[3])
    line_step(even, even_right, even_left, 0, even_view)
    line_step(odd, odd_right, odd_left, 2, odd_view)
    pl.when(odd)(odd_x.copy.start)
    line_step(even, even_right, even_left, 1, even_view)

    hid_far_sib.arrived()
    for t in range(TILES):
        part_far[t] = product(far[0], t).astype(jnp.bfloat16)
        far_sites[t].start()
    hid_far_same.arrived()
    for t in range(TILES):
        mine = product(far[1], t)
        far_sites[t].arrived()
        part_y[t] = (mine + got_far[t].astype(jnp.float32)).astype(jnp.bfloat16)
        y_sites[t].start()

    line_step(even, even_right, even_left, 2, even_view)

    def odd_take():
        odd_x.arrived()
        add(picked.at[z, x], from_x.at[0])

    pl.when(odd)(odd_take)

    quarter_sites = [
        Site(None, picked.at[z, x, (r + s) % QUARTERS], quarters.at[s], (v, (r + s) % QUARTERS))
        for s in range(1, QUARTERS)
    ]
    for site in quarter_sites:
        site.start()
    whole = emb.at[z, x]

    def place(q, block):
        for k in range(QUARTERS):
            @pl.when(q == k)
            def _(k=k):
                whole[:, k * depth:(k + 1) * depth] = block

    place(r, picked[z, x, r])
    for s, site in enumerate(quarter_sites, 1):
        site.arrived()
        place((r + QUARTERS - s) % QUARTERS, quarters[s])

    go_right, go_left, go_x = {}, {}, {}
    for j in range(LINE):
        for xx in range(2):
            mine = jnp.logical_or(odd, x == xx)
            src = emb.at[j, xx]
            go_right[j, xx] = Site(both(mine, z >= j, z < LINE - 1), src, src, (right, r))
            go_left[j, xx] = Site(both(mine, z <= j, z > 0), src, src, (left, r))
            go_x[j, xx] = Site(both(x == xx, jnp.logical_or(even, z == j)), src, src, (other_x, r))

    def each(j, cond, action):
        for xx in range(2):
            pl.when(both(cond, z == j, xx == x))(functools.partial(action, j, xx))

    for j in range(LINE):
        for xx in range(2):
            here = both(z == j, x == xx)
            for group_of in (go_right, go_left, go_x):
                site = group_of[j, xx]
                pl.when(both(here, site.cond))(site.copy.start)
    for j in range(LINE):
        for xx in range(2):
            there = both(odd, z == j, x == 1 - xx)

            def from_neighbour(j=j, xx=xx):
                go_x[j, xx].arrived()

            pl.when(there)(from_neighbour)
            for group_of in (go_right, go_left):
                site = group_of[j, xx]
                pl.when(both(there, site.cond))(site.copy.start)

    def gather_step(d):
        for j in range(LINE):
            for xx in range(2):
                mine = jnp.logical_or(odd, x == xx)
                if j + d < LINE:
                    at = both(mine, z == j + d)
                    pl.when(at)(go_right[j, xx].arrived)
                    pl.when(both(at, go_right[j, xx].cond))(go_right[j, xx].copy.start)
                    pl.when(both(at, go_x[j, xx].cond))(go_x[j, xx].copy.start)
                if j - d >= 0:
                    at = both(mine, z == j - d)
                    pl.when(at)(go_left[j, xx].arrived)
                    pl.when(both(at, go_left[j, xx].cond))(go_left[j, xx].copy.start)
                    pl.when(both(at, go_x[j, xx].cond))(go_x[j, xx].copy.start)

    near_products()
    gather_step(1)

    sum_e[...] = jnp.zeros_like(sum_e)
    sum_c[...] = jnp.zeros_like(sum_c)
    some = 32
    out_copies = []

    def cap_tile(t):
        near_sites[t].arrived()
        y_sites[t].arrived()

        def cap_step(i, _):
            at = pl.ds(pl.multiple_of(i * some, some), some)
            logits = own[t, at, :] + got_near[t, at, :].astype(jnp.float32)
            logits = logits + got_y[t, at, :].astype(jnp.float32)
            capped = soft_cap * jnp.tanh(logits / soft_cap)
            cap[at, t * width:(t + 1) * width] = capped
            exps = jnp.exp(capped)
            about = tok_t[r, at, :]
            parent = about[:, 1:2].reshape(some // BEAMS, BEAMS, 1)
            beams = capped.reshape(some // BEAMS, BEAMS, width)
            chosen = jnp.zeros_like(beams)
            for b in range(BEAMS):
                chosen = jnp.where(parent == float(b), beams[:, b:b + 1, :], chosen)
            entry = lax.broadcasted_iota(jnp.int32, (some, width), 1) + t * width
            hit = entry.astype(jnp.float32) == about[:, 0:1] - base
            chosen = jnp.where(hit, chosen.reshape(some, width), 0.0)
            for k in range(0, width, 128):
                sum_e[at, :] += exps[:, k:k + 128]
                sum_c[at, :] += chosen[:, k:k + 128]
            return 0

        lax.fori_loop(0, rows // some, cap_step, 0)
        span = pl.ds(t * width, width)
        copy = pltpu.make_async_copy(cap.at[:, span], cap_out.at[:, span], out_sem.at[t])
        copy.start()
        out_copies.append(copy)

    cap_tile(0)
    cap_tile(1)
    gather_step(2)
    cap_tile(2)
    cap_tile(3)
    lane = lax.broadcasted_iota(jnp.int32, (rows, 128), 1)
    total_e = jnp.sum(sum_e[...], axis=1, keepdims=True)
    total_c = jnp.sum(sum_c[...], axis=1, keepdims=True)
    mine = tok_t[r]
    parent = mine[:, 1:2].reshape(rows // BEAMS, BEAMS, 1)

    def of_parent(column):
        beams = column.reshape(rows // BEAMS, BEAMS, 1)
        found = jnp.zeros_like(beams)
        for b in range(BEAMS):
            found = jnp.where(parent == float(b), beams[:, b:b + 1, :], found)
        return found.reshape(rows, 1)

    parent_e = of_parent(total_e)
    parent_score = of_parent(mine[:, 2:3])
    stat = jnp.where(lane == 0, total_e, jnp.where(lane == 1, total_c, jnp.where(lane == 2, parent_e, 0.0))).T[:8]
    scores = jnp.where(lane == 3, parent_score, 0.0).T[:8]
    stat_in[0] = stat
    stat_sites = [Site(None, stat_in.at[0], stat_in.at[s], ((v + s) % shards, r)) for s in range(1, shards)]
    for site in stat_sites:
        site.start()

    gather_step(3)
    for j in range(LINE):
        for xx in range(2):
            pl.when(both(even, x == 1 - xx))(go_x[j, xx].arrived)
    emb_copy = pltpu.make_async_copy(emb, emb_out, out_sem.at[TILES])
    emb_copy.start()
    for s, site in enumerate(stat_sites, 1):
        site.arrived()
        stat = stat + stat_in[s]
    stat_out[...] = stat + scores
    for site in sites:
        site.sent()
    for copy in out_copies:
        copy.wait()
    emb_copy.wait()


def fused(hidden, norm_gain, embed_table, tokens, parents, prev_scores, lengths):
    shards = 2 * LINE
    voc_rows, depth = embed_table.shape
    rows, features = hidden.shape
    piece = rows // shards
    width = voc_rows // TILES
    line_of = lax.broadcasted_iota(jnp.int32, (8, rows), 0)
    aux = jnp.where(line_of == 0, tokens.astype(jnp.float32)[None], prev_scores[None])
    aux = jnp.where(line_of == 1, parents.astype(jnp.float32)[None], aux)
    half, full = jnp.bfloat16, jnp.float32
    anywhere, vmem = pl.BlockSpec(memory_space=pl.ANY), pl.BlockSpec(memory_space=pltpu.VMEM)
    tiles = pltpu.VMEM((TILES, rows, width), half)
    line = pltpu.VMEM((LINE, 2, QUARTERS, piece, depth), half)
    capped, stat, raw = pl.pallas_call(
        kernel,
        out_shape=(
            jax.ShapeDtypeStruct((rows, voc_rows), full),
            jax.ShapeDtypeStruct((8, rows), full),
            jax.ShapeDtypeStruct((LINE, 2, piece, features), half),
        ),
        in_specs=[anywhere, vmem, anywhere, vmem],
        out_specs=(anywhere, vmem, anywhere),
        scratch_shapes=[
            pltpu.VMEM((rows, features), half),
            pltpu.VMEM((voc_rows, depth), half),
            pltpu.VMEM((QUARTERS, rows, depth), half),
            pltpu.VMEM((3, rows, depth), half),
            pltpu.VMEM((QUARTERS, 8, rows), full),
            pltpu.VMEM((QUARTERS, rows, 128), full),
            pltpu.VMEM((LINE, 2, QUARTERS, piece, 128), full),
            pltpu.VMEM((2 * QUARTERS * piece, depth), full),
            line,
            line,
            line,
            pltpu.VMEM((LINE, QUARTERS, piece, depth), half),
            pltpu.VMEM((QUARTERS, piece, depth), half),
            pltpu.VMEM((LINE, 2, piece, features), half),
            pltpu.VMEM((TILES, rows, width), full),
            tiles, tiles, tiles, tiles, tiles, tiles,
            pltpu.VMEM((rows, voc_rows), full),
            pltpu.VMEM((rows, 128), full),
            pltpu.VMEM((rows, 128), full),
            pltpu.VMEM((shards, 8, rows), full),
            pltpu.SemaphoreType.DMA((2,)),
            pltpu.SemaphoreType.DMA((TILES + 1,)),
            pltpu.SemaphoreType.DMA((80,)),
            pltpu.SemaphoreType.DMA((80,)),
        ],
        compiler_params=pltpu.CompilerParams(
            collective_id=0, has_side_effects=True, vmem_limit_bytes=58 * 2**20
        ),
        cost_estimate=pl.CostEstimate(
            flops=8 * rows * QUARTERS // 2 * voc_rows * depth, bytes_accessed=12 * 2**20,
            transcendentals=2 * rows * voc_rows,
        ),
    )(hidden, norm_gain, embed_table, aux)
    lse = jnp.log(stat[0])
    log_probs = capped - lse[:, None]
    chosen_lp = stat[1] - jnp.log(stat[2])
    penalty = jnp.power((5.0 + lengths.astype(full)) / 6.0, length_power)
    normalized = (stat[3] + chosen_lp) / penalty
    next_embed = (raw.reshape(rows, features).astype(full) * math.sqrt(features)).astype(half)
    return (log_probs, chosen_lp, normalized, next_embed)


def solution(mesh):
    placed = (P("rows", None), P(), P("vocab", "rows"), P("rows"), P("rows"), P("rows"), P("rows"))
    shards = mesh.shape["vocab"]
    fits = shards == 2 * LINE and mesh.shape["rows"] == QUARTERS
    return jax.shard_map(
        fused if fits else functools.partial(plain, shards),
        mesh=mesh,
        in_specs=placed,
        out_specs=(P("rows", "vocab"), P("rows"), P("rows"), P("rows", None)),
        check_vma=False,
    )
```

```python
import functools
import math

import jax
import jax.numpy as jnp
from jax import lax
from jax.experimental import pallas as pl
from jax.experimental.pallas import tpu as pltpu
from jax.sharding import PartitionSpec as P

BEAMS = 8


soft_cap = 30.0
length_power = 0.6
norm_eps = 1e-06


def by_parent(values, parents):
    groups = values.reshape(-1, 1, BEAMS)
    hit = parents.reshape(-1, BEAMS, 1) == jnp.arange(BEAMS, dtype=jnp.int32)
    return jnp.sum(jnp.where(hit, groups, 0.0), axis=2).reshape(-1)


def plain(shards, hidden, norm_gain, embed_table, tokens, parents, prev_scores, lengths):
    shard_index = lax.axis_index("vocab")
    voc_rows = embed_table.shape[0]
    row_count, width = hidden.shape
    scale = math.sqrt(width)

    all_tokens = lax.all_gather(tokens, "rows", axis=0, tiled=False)
    groups = all_tokens.shape[0]
    piece = row_count // shards
    order = all_tokens.reshape(groups, shards, piece).transpose(1, 0, 2).reshape(-1)
    all_col = order - shard_index * voc_rows
    all_inside = (all_col >= 0) & (all_col < voc_rows)
    picked = jnp.take(embed_table, jnp.clip(all_col, 0, voc_rows - 1), axis=0)
    picked = jnp.where(all_inside[:, None], picked, jnp.zeros((), jnp.bfloat16))
    summed = lax.psum_scatter(picked, "vocab", scatter_dimension=0, tiled=True)

    states = hidden.astype(jnp.float32)
    meansq = jnp.mean(states * states, axis=-1, keepdims=True)
    normed = (states * lax.rsqrt(meansq + norm_eps) * norm_gain.astype(jnp.float32)).astype(
        jnp.bfloat16
    )
    feature_cols = lax.all_to_all(normed, "rows", split_axis=1, concat_axis=0, tiled=True)
    logits = lax.psum_scatter(
        lax.dot_general(
            feature_cols, embed_table, (((1,), (1,)), ((), ())), preferred_element_type=jnp.float32
        ).astype(jnp.bfloat16),
        "rows",
        scatter_dimension=0,
        tiled=True,
    ).astype(jnp.float32)

    quarter = lax.all_to_all(summed, "rows", split_axis=0, concat_axis=1, tiled=True)
    quarter = (quarter.astype(jnp.float32) * scale).astype(jnp.bfloat16)
    next_embed = lax.all_gather(quarter, "vocab", axis=0, tiled=True)

    local_col = tokens - shard_index * voc_rows
    inside = (local_col >= 0) & (local_col < voc_rows)
    clipped_col = jnp.clip(local_col, 0, voc_rows - 1)
    capped = soft_cap * jnp.tanh(logits / soft_cap)
    sum_exp = jnp.sum(jnp.exp(capped), axis=1)
    parent_rows = jnp.arange(row_count, dtype=jnp.int32) // BEAMS * BEAMS + parents
    chosen_local = jnp.where(inside, capped[parent_rows, clipped_col], 0.0)
    total_exp, chosen_logit = lax.psum((sum_exp, chosen_local), "vocab")
    lse = jnp.log(total_exp)
    log_probs = capped - lse[:, None]
    chosen_lp = chosen_logit - by_parent(lse, parents)
    penalty = jnp.power((5.0 + lengths.astype(jnp.float32)) / 6.0, length_power)
    normalized = (by_parent(prev_scores, parents) + chosen_lp) / penalty
    return (log_probs, chosen_lp, normalized, next_embed)


LINE = 4
QUARTERS = 4
TILES = 4
DEPTH = 512


def kernel(
    hidden_ref, gain_ref, table_ref, aux_ref, cap_out, stat_out, emb_out,
    hid, table, nrm, far, aux_in, tok_t, tok_p, acc, picked, from_z, from_x,
    quarters, emb, own, part_near, part_far, part_y, got_near, got_far, got_y, cap,
    sum_e, sum_c, stat_in, load_sem, out_sem, send_sem, recv_sem,
):
    v, r = lax.axis_index("vocab"), lax.axis_index("rows")
    z, x, y, c = v // 2, v % 2, r // 2, r % 2
    shards = 2 * LINE
    other_x = z * 2 + (1 - x)
    sib = y * 2 + (1 - c)
    far_same = (1 - y) * 2 + c
    far_sib = (1 - y) * 2 + (1 - c)
    voc_rows, depth = table.shape
    rows = hid.shape[0]
    piece = rows // shards
    width = voc_rows // TILES

    sites = []

    class Site:
        def __init__(self, src, dst, device):
            k = len(sites)
            sites.append(self)
            self.copy = pltpu.make_async_remote_copy(
                src_ref=src, dst_ref=dst, send_sem=send_sem.at[k], recv_sem=recv_sem.at[k],
                device_id=device, device_id_type=pl.DeviceIdType.MESH,
            )

        def start(self):
            self.copy.start()

        def sent(self):
            self.copy.wait_send()

        def arrived(self):
            self.copy.wait_recv()

    load_hidden = pltpu.make_async_copy(hidden_ref, hid, load_sem.at[0])
    load_table = pltpu.make_async_copy(table_ref, table, load_sem.at[1])
    load_hidden.start()
    load_table.start()

    barrier = pltpu.get_barrier_semaphore()
    for step in range(1, QUARTERS):
        pl.semaphore_signal(barrier, inc=1, device_id=(v, (r + step) % QUARTERS),
                            device_id_type=pl.DeviceIdType.MESH)
    for step in range(1, shards):
        pl.semaphore_signal(barrier, inc=1, device_id=((v + step) % shards, r),
                            device_id_type=pl.DeviceIdType.MESH)
    pl.semaphore_wait(barrier, QUARTERS + shards - 2)

    aux_sites = [Site(aux_ref, aux_in.at[s], (v, (r + s) % QUARTERS)) for s in range(1, QUARTERS)]
    for site in aux_sites:
        site.start()

    load_hidden.wait()
    gain = gain_ref[...].astype(jnp.float32).reshape(1, QUARTERS * depth)

    def norm_step(i, _):
        at = pl.ds(pl.multiple_of(i * 16, 16), 16)
        states = hid[at, :].astype(jnp.float32)
        meansq = jnp.mean(states * states, axis=-1, keepdims=True)
        normed = (states * lax.rsqrt(meansq + norm_eps) * gain).astype(jnp.bfloat16)
        for q in range(QUARTERS):
            nrm[q, at, :] = normed[:, q * depth:(q + 1) * depth]
        return 0

    lax.fori_loop(0, rows // 16, norm_step, 0)
    hid_far_sib = Site(nrm.at[far_sib], far.at[0], (v, far_sib))
    hid_far_same = Site(nrm.at[far_same], far.at[1], (v, far_same))
    hid_sib = Site(nrm.at[sib], far.at[2], (v, sib))
    hid_sib.start()
    hid_far_sib.start()
    hid_far_same.start()

    def columns(block):
        return jnp.concatenate([block] * (128 // 8), axis=0).T

    tok_t[r] = columns(aux_ref[...])
    for s, site in enumerate(aux_sites, 1):
        site.arrived()
        tok_t[(r + QUARTERS - s) % QUARTERS] = columns(aux_in[s])
    for p in range(shards):
        for q in range(QUARTERS):
            tok_p[p // 2, p % 2, q] = tok_t[q, p * piece:(p + 1) * piece, :]
    load_table.wait()

    base = (v * voc_rows).astype(jnp.float32)
    group = QUARTERS * piece

    def lookup(za, xa, zb, xb):
        tok = jnp.concatenate(
            [tok_p[za, xa].reshape(group, 128), tok_p[zb, xb].reshape(group, 128)], axis=0
        )[:, :1] - base

        def step(k, _):
            entry = lax.broadcasted_iota(jnp.int32, (2 * group, DEPTH), 1) + k * DEPTH
            hot = jnp.where(entry.astype(jnp.float32) == tok, 1.0, 0.0).astype(jnp.bfloat16)
            at = pl.ds(pl.multiple_of(k * DEPTH, DEPTH), DEPTH)
            acc[...] += jnp.dot(hot, table[at, :], preferred_element_type=jnp.float32)
            return 0

        acc[...] = jnp.zeros_like(acc)
        lax.fori_loop(0, voc_rows // DEPTH, step, 0)
        for half, (zz, xx) in enumerate(((za, xa), (zb, xb))):
            block = acc[half * group:(half + 1) * group, :].astype(jnp.bfloat16)
            picked[zz, xx] = block.reshape(QUARTERS, piece, depth)

    places = (LINE - 1 - z, (z + LINE // 2) % LINE, z + 1 - 2 * (z % 2), z)
    across = [Site(picked.at[j, 1 - x], from_x.at[k], (other_x, r)) for k, j in enumerate(places)]
    along = [Site(picked.at[j, x], from_z.at[k], (j * 2 + x, r)) for k, j in enumerate(places[:-1])]

    def add(dst, src):
        def one(i, _):
            dst[i] = dst[i] + src[i]
            return 0

        lax.fori_loop(0, QUARTERS, one, 0)

    def take(k):
        across[k].arrived()
        add(picked.at[places[k], x], from_x.at[k])
        if k < LINE - 1:
            along[k].start()

    for xx in (1 - x, x):
        for k in (0, 2):
            lookup(places[k], xx, places[k + 1], xx)
            if xx is not x:
                across[k].start()
                across[k + 1].start()

    def product(block, t):
        at = pl.ds(pl.multiple_of(t * width, width), width)
        return lax.dot_general(block, table[at, :], (((1,), (1,)), ((), ())),
                               preferred_element_type=jnp.float32)

    near_sites = [Site(part_near.at[t], got_near.at[t], (v, sib)) for t in range(TILES)]
    far_sites = [Site(part_far.at[t], got_far.at[t], (v, sib)) for t in range(TILES)]
    y_sites = [Site(part_y.at[t], got_y.at[t], (v, far_same)) for t in range(TILES)]

    take(0)

    def own_step(t, _):
        own[t] = product(nrm[r], t)
        return 0

    lax.fori_loop(0, TILES, own_step, 0)
    take(1)
    hid_sib.arrived()
    for t in range(TILES):
        part_near[t] = product(far[2], t).astype(jnp.bfloat16)
        near_sites[t].start()
    take(2)
    hid_far_sib.arrived()
    for t in range(TILES):
        part_far[t] = product(far[0], t).astype(jnp.bfloat16)
        far_sites[t].start()
    take(3)
    hid_far_same.arrived()
    for t in range(TILES):
        mine = product(far[1], t)
        far_sites[t].arrived()
        part_y[t] = (mine + got_far[t].astype(jnp.float32)).astype(jnp.bfloat16)
        y_sites[t].start()
    for k, site in enumerate(along):
        site.arrived()
        add(picked.at[z, x], from_z.at[k])

    quarter_sites = [
        Site(picked.at[z, x, (r + s) % QUARTERS], quarters.at[s], (v, (r + s) % QUARTERS))
        for s in range(1, QUARTERS)
    ]
    for site in quarter_sites:
        site.start()
    whole = emb.at[z, x]

    def place(q, block):
        for k in range(QUARTERS):
            @pl.when(q == k)
            def _(k=k):
                whole[:, k * depth:(k + 1) * depth] = block

    place(r, picked[z, x, r])
    for s, site in enumerate(quarter_sites, 1):
        site.arrived()
        place((r + QUARTERS - s) % QUARTERS, quarters[s])

    def piece_site(j, device):
        at = emb.at[j, x]
        return Site(at, at, (device, r))

    give = [piece_site(z, j * 2 + x) for j in places[:-1]]
    hand = [piece_site(j, other_x) for j in places]
    for k in (0, 1, 2):
        give[k].start()
    hand[LINE - 1].start()

    def gather_step(k):
        give[k].arrived()
        hand[k].start()

    gather_step(2)
    gather_step(0)

    sum_e[...] = jnp.zeros_like(sum_e)
    sum_c[...] = jnp.zeros_like(sum_c)
    some = 32
    out_copies = []

    def cap_tile(t):
        near_sites[t].arrived()
        y_sites[t].arrived()

        def cap_step(i, _):
            at = pl.ds(pl.multiple_of(i * some, some), some)
            logits = own[t, at, :] + got_near[t, at, :].astype(jnp.float32)
            logits = logits + got_y[t, at, :].astype(jnp.float32)
            capped = soft_cap * jnp.tanh(logits / soft_cap)
            cap[at, t * width:(t + 1) * width] = capped
            exps = jnp.exp(capped)
            about = tok_t[r, at, :]
            parent = about[:, 1:2].reshape(some // BEAMS, BEAMS, 1)
            beams = capped.reshape(some // BEAMS, BEAMS, width)
            chosen = jnp.zeros_like(beams)
            for b in range(BEAMS):
                chosen = jnp.where(parent == float(b), beams[:, b:b + 1, :], chosen)
            entry = lax.broadcasted_iota(jnp.int32, (some, width), 1) + t * width
            hit = entry.astype(jnp.float32) == about[:, 0:1] - base
            chosen = jnp.where(hit, chosen.reshape(some, width), 0.0)
            for k in range(0, width, 128):
                sum_e[at, :] += exps[:, k:k + 128]
                sum_c[at, :] += chosen[:, k:k + 128]
            return 0

        lax.fori_loop(0, rows // some, cap_step, 0)
        span = pl.ds(t * width, width)
        copy = pltpu.make_async_copy(cap.at[:, span], cap_out.at[:, span], out_sem.at[t])
        copy.start()
        out_copies.append(copy)

    for t in range(TILES):
        cap_tile(t)
    lane = lax.broadcasted_iota(jnp.int32, (rows, 128), 1)
    total_e = jnp.sum(sum_e[...], axis=1, keepdims=True)
    total_c = jnp.sum(sum_c[...], axis=1, keepdims=True)
    mine = tok_t[r]
    parent = mine[:, 1:2].reshape(rows // BEAMS, BEAMS, 1)

    def of_parent(column):
        beams = column.reshape(rows // BEAMS, BEAMS, 1)
        found = jnp.zeros_like(beams)
        for b in range(BEAMS):
            found = jnp.where(parent == float(b), beams[:, b:b + 1, :], found)
        return found.reshape(rows, 1)

    parent_e = of_parent(total_e)
    parent_score = of_parent(mine[:, 2:3])
    stat = jnp.where(lane == 0, total_e, jnp.where(lane == 1, total_c, jnp.where(lane == 2, parent_e, 0.0))).T[:8]
    scores = jnp.where(lane == 3, parent_score, 0.0).T[:8]
    stat_in[0] = stat
    stat_sites = [Site(stat_in.at[0], stat_in.at[s], ((v + s) % shards, r)) for s in range(1, shards)]
    for site in stat_sites:
        site.start()

    gather_step(1)
    for site in hand:
        site.arrived()
    emb_copy = pltpu.make_async_copy(emb, emb_out, out_sem.at[TILES])
    emb_copy.start()
    for s, site in enumerate(stat_sites, 1):
        site.arrived()
        stat = stat + stat_in[s]
    stat_out[...] = stat + scores
    for site in sites:
        site.sent()
    for copy in out_copies:
        copy.wait()
    emb_copy.wait()


def fused(hidden, norm_gain, embed_table, tokens, parents, prev_scores, lengths):
    shards = 2 * LINE
    voc_rows, depth = embed_table.shape
    rows, features = hidden.shape
    piece = rows // shards
    width = voc_rows // TILES
    line_of = lax.broadcasted_iota(jnp.int32, (8, rows), 0)
    aux = jnp.where(line_of == 0, tokens.astype(jnp.float32)[None], prev_scores[None])
    aux = jnp.where(line_of == 1, parents.astype(jnp.float32)[None], aux)
    half, full = jnp.bfloat16, jnp.float32
    anywhere, vmem = pl.BlockSpec(memory_space=pl.ANY), pl.BlockSpec(memory_space=pltpu.VMEM)
    tiles = pltpu.VMEM((TILES, rows, width), half)
    line = pltpu.VMEM((LINE, 2, QUARTERS, piece, depth), half)
    capped, stat, raw = pl.pallas_call(
        kernel,
        out_shape=(
            jax.ShapeDtypeStruct((rows, voc_rows), full),
            jax.ShapeDtypeStruct((8, rows), full),
            jax.ShapeDtypeStruct((LINE, 2, piece, features), half),
        ),
        in_specs=[anywhere, vmem, anywhere, vmem],
        out_specs=(anywhere, vmem, anywhere),
        scratch_shapes=[
            pltpu.VMEM((rows, features), half),
            pltpu.VMEM((voc_rows, depth), half),
            pltpu.VMEM((QUARTERS, rows, depth), half),
            pltpu.VMEM((3, rows, depth), half),
            pltpu.VMEM((QUARTERS, 8, rows), full),
            pltpu.VMEM((QUARTERS, rows, 128), full),
            pltpu.VMEM((LINE, 2, QUARTERS, piece, 128), full),
            pltpu.VMEM((2 * QUARTERS * piece, depth), full),
            line,
            pltpu.VMEM((LINE - 1, QUARTERS, piece, depth), half),
            pltpu.VMEM((LINE, QUARTERS, piece, depth), half),
            pltpu.VMEM((QUARTERS, piece, depth), half),
            pltpu.VMEM((LINE, 2, piece, features), half),
            pltpu.VMEM((TILES, rows, width), full),
            tiles, tiles, tiles, tiles, tiles, tiles,
            pltpu.VMEM((rows, voc_rows), full),
            pltpu.VMEM((rows, 128), full),
            pltpu.VMEM((rows, 128), full),
            pltpu.VMEM((shards, 8, rows), full),
            pltpu.SemaphoreType.DMA((2,)),
            pltpu.SemaphoreType.DMA((TILES + 1,)),
            pltpu.SemaphoreType.DMA((80,)),
            pltpu.SemaphoreType.DMA((80,)),
        ],
        compiler_params=pltpu.CompilerParams(
            collective_id=0, has_side_effects=True, vmem_limit_bytes=58 * 2**20
        ),
        cost_estimate=pl.CostEstimate(
            flops=8 * rows * QUARTERS // 2 * voc_rows * depth, bytes_accessed=12 * 2**20,
            transcendentals=2 * rows * voc_rows,
        ),
    )(hidden, norm_gain, embed_table, aux)
    lse = jnp.log(stat[0])
    log_probs = capped - lse[:, None]
    chosen_lp = stat[1] - jnp.log(stat[2])
    penalty = jnp.power((5.0 + lengths.astype(full)) / 6.0, length_power)
    normalized = (stat[3] + chosen_lp) / penalty
    next_embed = (raw.reshape(rows, features).astype(full) * math.sqrt(features)).astype(half)
    return (log_probs, chosen_lp, normalized, next_embed)


def solution(mesh):
    placed = (P("rows", None), P(), P("vocab", "rows"), P("rows"), P("rows"), P("rows"), P("rows"))
    shards = mesh.shape["vocab"]
    fits = shards == 2 * LINE and mesh.shape["rows"] == QUARTERS
    return jax.shard_map(
        fused if fits else functools.partial(plain, shards),
        mesh=mesh,
        in_specs=placed,
        out_specs=(P("rows", "vocab"), P("rows"), P("rows"), P("rows", None)),
        check_vma=False,
    )
```

```python
import functools
import math

import jax
import jax.numpy as jnp
from jax import lax
from jax.experimental import pallas as pl
from jax.experimental.pallas import tpu as pltpu
from jax.sharding import PartitionSpec as P

BEAMS = 8


soft_cap = 30.0
length_power = 0.6
norm_eps = 1e-06


def by_parent(values, parents):
    groups = values.reshape(-1, 1, BEAMS)
    hit = parents.reshape(-1, BEAMS, 1) == jnp.arange(BEAMS, dtype=jnp.int32)
    return jnp.sum(jnp.where(hit, groups, 0.0), axis=2).reshape(-1)


def plain(shards, hidden, norm_gain, embed_table, tokens, parents, prev_scores, lengths):
    shard_index = lax.axis_index("vocab")
    voc_rows = embed_table.shape[0]
    row_count, width = hidden.shape
    scale = math.sqrt(width)

    all_tokens = lax.all_gather(tokens, "rows", axis=0, tiled=False)
    groups = all_tokens.shape[0]
    piece = row_count // shards
    order = all_tokens.reshape(groups, shards, piece).transpose(1, 0, 2).reshape(-1)
    all_col = order - shard_index * voc_rows
    all_inside = (all_col >= 0) & (all_col < voc_rows)
    picked = jnp.take(embed_table, jnp.clip(all_col, 0, voc_rows - 1), axis=0)
    picked = jnp.where(all_inside[:, None], picked, jnp.zeros((), jnp.bfloat16))
    summed = lax.psum_scatter(picked, "vocab", scatter_dimension=0, tiled=True)

    states = hidden.astype(jnp.float32)
    meansq = jnp.mean(states * states, axis=-1, keepdims=True)
    normed = (states * lax.rsqrt(meansq + norm_eps) * norm_gain.astype(jnp.float32)).astype(
        jnp.bfloat16
    )
    feature_cols = lax.all_to_all(normed, "rows", split_axis=1, concat_axis=0, tiled=True)
    logits = lax.psum_scatter(
        lax.dot_general(
            feature_cols, embed_table, (((1,), (1,)), ((), ())), preferred_element_type=jnp.float32
        ).astype(jnp.bfloat16),
        "rows",
        scatter_dimension=0,
        tiled=True,
    ).astype(jnp.float32)

    quarter = lax.all_to_all(summed, "rows", split_axis=0, concat_axis=1, tiled=True)
    quarter = (quarter.astype(jnp.float32) * scale).astype(jnp.bfloat16)
    next_embed = lax.all_gather(quarter, "vocab", axis=0, tiled=True)

    local_col = tokens - shard_index * voc_rows
    inside = (local_col >= 0) & (local_col < voc_rows)
    clipped_col = jnp.clip(local_col, 0, voc_rows - 1)
    capped = soft_cap * jnp.tanh(logits / soft_cap)
    sum_exp = jnp.sum(jnp.exp(capped), axis=1)
    parent_rows = jnp.arange(row_count, dtype=jnp.int32) // BEAMS * BEAMS + parents
    chosen_local = jnp.where(inside, capped[parent_rows, clipped_col], 0.0)
    total_exp, chosen_logit = lax.psum((sum_exp, chosen_local), "vocab")
    lse = jnp.log(total_exp)
    log_probs = capped - lse[:, None]
    chosen_lp = chosen_logit - by_parent(lse, parents)
    penalty = jnp.power((5.0 + lengths.astype(jnp.float32)) / 6.0, length_power)
    normalized = (by_parent(prev_scores, parents) + chosen_lp) / penalty
    return (log_probs, chosen_lp, normalized, next_embed)


LINE = 4
QUARTERS = 4
TILES = 4
DEPTH = 512


def kernel(
    hidden_ref, gain_ref, table_ref, tokens_ref, parents_ref, scores_ref, cap_out, stat_out, emb_out,
    hid, table, nrm, far, aux, aux_in, tok_t, tok_p, acc, picked, from_z, from_x,
    quarters, emb, own, part_near, part_far, part_y, got_near, got_far, got_y, cap,
    sum_e, sum_c, stat_in, load_sem, out_sem, send_sem, recv_sem,
):
    v, r = lax.axis_index("vocab"), lax.axis_index("rows")
    z, x, y, c = v // 2, v % 2, r // 2, r % 2
    shards = 2 * LINE
    other_x = z * 2 + (1 - x)
    sib = y * 2 + (1 - c)
    far_same = (1 - y) * 2 + c
    far_sib = (1 - y) * 2 + (1 - c)
    voc_rows, depth = table.shape
    rows = hid.shape[0]
    piece = rows // shards
    width = voc_rows // TILES

    sites = []

    class Site:
        def __init__(self, src, dst, device):
            k = len(sites)
            sites.append(self)
            self.copy = pltpu.make_async_remote_copy(
                src_ref=src, dst_ref=dst, send_sem=send_sem.at[k], recv_sem=recv_sem.at[k],
                device_id=device, device_id_type=pl.DeviceIdType.MESH,
            )

        def start(self):
            self.copy.start()

        def sent(self):
            self.copy.wait_send()

        def arrived(self):
            self.copy.wait_recv()

    row_of = lax.broadcasted_iota(jnp.int32, (8, rows), 0)
    about = jnp.where(row_of == 0, tokens_ref[...].reshape(1, rows), parents_ref[...].reshape(1, rows))
    aux[...] = jnp.where(row_of < 2, about.astype(jnp.float32), scores_ref[...].reshape(1, rows))
    load_hidden = pltpu.make_async_copy(hidden_ref, hid, load_sem.at[0])
    load_table = pltpu.make_async_copy(table_ref, table, load_sem.at[1])
    load_hidden.start()
    load_table.start()

    barrier = pltpu.get_barrier_semaphore()
    for step in range(1, QUARTERS):
        pl.semaphore_signal(barrier, inc=1, device_id=(v, (r + step) % QUARTERS),
                            device_id_type=pl.DeviceIdType.MESH)
    for step in range(1, shards):
        pl.semaphore_signal(barrier, inc=1, device_id=((v + step) % shards, r),
                            device_id_type=pl.DeviceIdType.MESH)
    pl.semaphore_wait(barrier, QUARTERS + shards - 2)

    aux_sites = [Site(aux, aux_in.at[s], (v, (r + s) % QUARTERS)) for s in range(1, QUARTERS)]
    for site in aux_sites:
        site.start()

    load_hidden.wait()
    gain = gain_ref[...].astype(jnp.float32).reshape(1, QUARTERS * depth)

    def norm_step(i, _):
        at = pl.ds(pl.multiple_of(i * 16, 16), 16)
        states = hid[at, :].astype(jnp.float32)
        meansq = jnp.mean(states * states, axis=-1, keepdims=True)
        normed = (states * lax.rsqrt(meansq + norm_eps) * gain).astype(jnp.bfloat16)
        for q in range(QUARTERS):
            nrm[q, at, :] = normed[:, q * depth:(q + 1) * depth]
        return 0

    lax.fori_loop(0, rows // 16, norm_step, 0)
    hid_far_sib = Site(nrm.at[far_sib], far.at[0], (v, far_sib))
    hid_far_same = Site(nrm.at[far_same], far.at[1], (v, far_same))
    hid_sib = Site(nrm.at[sib], far.at[2], (v, sib))
    hid_sib.start()
    hid_far_sib.start()
    hid_far_same.start()

    def columns(block):
        return jnp.concatenate([block] * (128 // 8), axis=0).T

    tok_t[r] = columns(aux[...])
    for s, site in enumerate(aux_sites, 1):
        site.arrived()
        tok_t[(r + QUARTERS - s) % QUARTERS] = columns(aux_in[s])
    for p in range(shards):
        for q in range(QUARTERS):
            tok_p[p // 2, p % 2, q] = tok_t[q, p * piece:(p + 1) * piece, :]
    load_table.wait()

    base = (v * voc_rows).astype(jnp.float32)
    group = QUARTERS * piece

    def lookup(za, xa, zb, xb):
        tok = jnp.concatenate(
            [tok_p[za, xa].reshape(group, 128), tok_p[zb, xb].reshape(group, 128)], axis=0
        )[:, :1] - base

        def step(k, _):
            entry = lax.broadcasted_iota(jnp.int32, (2 * group, DEPTH), 1) + k * DEPTH
            hot = jnp.where(entry.astype(jnp.float32) == tok, 1.0, 0.0).astype(jnp.bfloat16)
            at = pl.ds(pl.multiple_of(k * DEPTH, DEPTH), DEPTH)
            acc[...] += jnp.dot(hot, table[at, :], preferred_element_type=jnp.float32)
            return 0

        acc[...] = jnp.zeros_like(acc)
        lax.fori_loop(0, voc_rows // DEPTH, step, 0)
        for half, (zz, xx) in enumerate(((za, xa), (zb, xb))):
            block = acc[half * group:(half + 1) * group, :].astype(jnp.bfloat16)
            picked[zz, xx] = block.reshape(QUARTERS, piece, depth)

    places = (LINE - 1 - z, (z + LINE // 2) % LINE, z + 1 - 2 * (z % 2), z)
    across = [Site(picked.at[j, 1 - x], from_x.at[k], (other_x, r)) for k, j in enumerate(places)]
    along = [Site(picked.at[j, x], from_z.at[k], (j * 2 + x, r)) for k, j in enumerate(places[:-1])]

    def add(dst, src):
        def one(i, _):
            dst[i] = dst[i] + src[i]
            return 0

        lax.fori_loop(0, QUARTERS, one, 0)

    def take(k):
        across[k].arrived()
        add(picked.at[places[k], x], from_x.at[k])
        if k < LINE - 1:
            along[k].start()

    for xx in (1 - x, x):
        for k in (0, 2):
            lookup(places[k], xx, places[k + 1], xx)
            if xx is not x:
                across[k].start()
                across[k + 1].start()

    def product(block, t):
        at = pl.ds(pl.multiple_of(t * width, width), width)
        return lax.dot_general(block, table[at, :], (((1,), (1,)), ((), ())),
                               preferred_element_type=jnp.float32)

    near_sites = [Site(part_near.at[t], got_near.at[t], (v, sib)) for t in range(TILES)]
    far_sites = [Site(part_far.at[t], got_far.at[t], (v, sib)) for t in range(TILES)]
    y_sites = [Site(part_y.at[t], got_y.at[t], (v, far_same)) for t in range(TILES)]

    take(0)

    def own_step(t, _):
        own[t] = product(nrm[r], t)
        return 0

    lax.fori_loop(0, TILES, own_step, 0)
    take(1)
    hid_sib.arrived()
    for t in range(TILES):
        part_near[t] = product(far[2], t).astype(jnp.bfloat16)
        near_sites[t].start()
    take(2)
    hid_far_sib.arrived()
    for t in range(TILES):
        part_far[t] = product(far[0], t).astype(jnp.bfloat16)
        far_sites[t].start()
    hid_far_same.arrived()
    for t in range(TILES):
        mine = product(far[1], t)
        far_sites[t].arrived()
        part_y[t] = (mine + got_far[t].astype(jnp.float32)).astype(jnp.bfloat16)
        if t < TILES // 2:
            y_sites[t].start()
    take(3)
    for k, site in enumerate(along):
        site.arrived()
        add(picked.at[z, x], from_z.at[k])

    quarter_sites = [
        Site(picked.at[z, x, (r + s) % QUARTERS], quarters.at[s], (v, (r + s) % QUARTERS))
        for s in range(1, QUARTERS)
    ]
    for site in quarter_sites:
        site.start()
    whole = emb.at[z, x]

    def place(q, block):
        for k in range(QUARTERS):
            @pl.when(q == k)
            def _(k=k):
                whole[:, k * depth:(k + 1) * depth] = block

    place(r, picked[z, x, r])
    for s, site in enumerate(quarter_sites, 1):
        site.arrived()
        place((r + QUARTERS - s) % QUARTERS, quarters[s])

    def piece_site(j, device):
        at = emb.at[j, x]
        return Site(at, at, (device, r))

    give = [piece_site(z, j * 2 + x) for j in places[:-1]]
    hand = [piece_site(j, other_x) for j in places]
    for k in (0, 1, 2):
        give[k].start()
    hand[LINE - 1].start()

    def gather_step(k):
        give[k].arrived()
        hand[k].start()

    for t in range(TILES // 2, TILES):
        y_sites[t].start()

    sum_e[...] = jnp.zeros_like(sum_e)
    sum_c[...] = jnp.zeros_like(sum_c)
    some = 32
    out_copies = []

    def cap_tile(t):
        near_sites[t].arrived()
        y_sites[t].arrived()

        def cap_step(i, _):
            at = pl.ds(pl.multiple_of(i * some, some), some)
            logits = own[t, at, :] + got_near[t, at, :].astype(jnp.float32)
            logits = logits + got_y[t, at, :].astype(jnp.float32)
            capped = soft_cap * jnp.tanh(logits / soft_cap)
            cap[at, t * width:(t + 1) * width] = capped
            exps = jnp.exp(capped)
            about = tok_t[r, at, :]
            parent = about[:, 1:2].reshape(some // BEAMS, BEAMS, 1)
            beams = capped.reshape(some // BEAMS, BEAMS, width)
            chosen = jnp.zeros_like(beams)
            for b in range(BEAMS):
                chosen = jnp.where(parent == float(b), beams[:, b:b + 1, :], chosen)
            entry = lax.broadcasted_iota(jnp.int32, (some, width), 1) + t * width
            hit = entry.astype(jnp.float32) == about[:, 0:1] - base
            chosen = jnp.where(hit, chosen.reshape(some, width), 0.0)
            for k in range(0, width, 128):
                sum_e[at, :] += exps[:, k:k + 128]
                sum_c[at, :] += chosen[:, k:k + 128]
            return 0

        lax.fori_loop(0, rows // some, cap_step, 0)
        span = pl.ds(t * width, width)
        copy = pltpu.make_async_copy(cap.at[:, span], cap_out.at[:, span], out_sem.at[t])
        copy.start()
        out_copies.append(copy)

    cap_tile(0)
    gather_step(2)
    cap_tile(1)
    gather_step(0)
    for t in range(TILES // 2, TILES):
        cap_tile(t)
    lane = lax.broadcasted_iota(jnp.int32, (rows, 128), 1)
    total_e = jnp.sum(sum_e[...], axis=1, keepdims=True)
    total_c = jnp.sum(sum_c[...], axis=1, keepdims=True)
    mine = tok_t[r]
    parent = mine[:, 1:2].reshape(rows // BEAMS, BEAMS, 1)

    def of_parent(column):
        beams = column.reshape(rows // BEAMS, BEAMS, 1)
        found = jnp.zeros_like(beams)
        for b in range(BEAMS):
            found = jnp.where(parent == float(b), beams[:, b:b + 1, :], found)
        return found.reshape(rows, 1)

    parent_e = of_parent(total_e)
    parent_score = of_parent(mine[:, 2:3])
    stat = jnp.where(lane == 0, total_e, jnp.where(lane == 1, total_c, jnp.where(lane == 2, parent_e, 0.0))).T[:8]
    scores = jnp.where(lane == 3, parent_score, 0.0).T[:8]
    stat_in[0] = stat
    stat_sites = [Site(stat_in.at[0], stat_in.at[s], ((v + s) % shards, r)) for s in range(1, shards)]
    for site in stat_sites:
        site.start()

    gather_step(1)
    for site in hand:
        site.arrived()
    emb_copy = pltpu.make_async_copy(emb, emb_out, out_sem.at[TILES])
    emb_copy.start()
    for s, site in enumerate(stat_sites, 1):
        site.arrived()
        stat = stat + stat_in[s]
    stat_out[...] = stat + scores
    for site in sites:
        site.sent()
    for copy in out_copies:
        copy.wait()
    emb_copy.wait()


def fused(hidden, norm_gain, embed_table, tokens, parents, prev_scores, lengths):
    shards = 2 * LINE
    voc_rows, depth = embed_table.shape
    rows, features = hidden.shape
    piece = rows // shards
    width = voc_rows // TILES
    half, full = jnp.bfloat16, jnp.float32
    anywhere, vmem = pl.BlockSpec(memory_space=pl.ANY), pl.BlockSpec(memory_space=pltpu.VMEM)
    stay = pl.BlockSpec(memory_space=pltpu.HBM)
    tiles = pltpu.VMEM((TILES, rows, width), half)
    line = pltpu.VMEM((LINE, 2, QUARTERS, piece, depth), half)
    capped, stat, raw = pl.pallas_call(
        kernel,
        out_shape=(
            jax.ShapeDtypeStruct((rows, voc_rows), full),
            jax.ShapeDtypeStruct((8, rows), full),
            jax.ShapeDtypeStruct((LINE, 2, piece, features), half),
        ),
        in_specs=[stay, vmem, stay, vmem, vmem, vmem],
        out_specs=(anywhere, vmem, anywhere),
        scratch_shapes=[
            pltpu.VMEM((rows, features), half),
            pltpu.VMEM((voc_rows, depth), half),
            pltpu.VMEM((QUARTERS, rows, depth), half),
            pltpu.VMEM((3, rows, depth), half),
            pltpu.VMEM((8, rows), full),
            pltpu.VMEM((QUARTERS, 8, rows), full),
            pltpu.VMEM((QUARTERS, rows, 128), full),
            pltpu.VMEM((LINE, 2, QUARTERS, piece, 128), full),
            pltpu.VMEM((2 * QUARTERS * piece, depth), full),
            line,
            pltpu.VMEM((LINE - 1, QUARTERS, piece, depth), half),
            pltpu.VMEM((LINE, QUARTERS, piece, depth), half),
            pltpu.VMEM((QUARTERS, piece, depth), half),
            pltpu.VMEM((LINE, 2, piece, features), half),
            pltpu.VMEM((TILES, rows, width), full),
            tiles, tiles, tiles, tiles, tiles, tiles,
            pltpu.VMEM((rows, voc_rows), full),
            pltpu.VMEM((rows, 128), full),
            pltpu.VMEM((rows, 128), full),
            pltpu.VMEM((shards, 8, rows), full),
            pltpu.SemaphoreType.DMA((2,)),
            pltpu.SemaphoreType.DMA((TILES + 1,)),
            pltpu.SemaphoreType.DMA((80,)),
            pltpu.SemaphoreType.DMA((80,)),
        ],
        compiler_params=pltpu.CompilerParams(
            collective_id=0, has_side_effects=True, vmem_limit_bytes=57 * 2**20
        ),
        cost_estimate=pl.CostEstimate(
            flops=8 * rows * QUARTERS // 2 * voc_rows * depth, bytes_accessed=12 * 2**20,
            transcendentals=2 * rows * voc_rows,
        ),
    )(hidden, norm_gain, embed_table, tokens, parents, prev_scores)
    lse = jnp.log(stat[0])
    log_probs = capped - lse[:, None]
    chosen_lp = stat[1] - jnp.log(stat[2])
    penalty = jnp.power((5.0 + lengths.astype(full)) / 6.0, length_power)
    normalized = (stat[3] + chosen_lp) / penalty
    next_embed = (raw.reshape(rows, features).astype(full) * math.sqrt(features)).astype(half)
    return (log_probs, chosen_lp, normalized, next_embed)


def solution(mesh):
    placed = (P("rows", None), P(), P("vocab", "rows"), P("rows"), P("rows"), P("rows"), P("rows"))
    shards = mesh.shape["vocab"]
    fits = shards == 2 * LINE and mesh.shape["rows"] == QUARTERS
    return jax.shard_map(
        fused if fits else functools.partial(plain, shards),
        mesh=mesh,
        in_specs=placed,
        out_specs=(P("rows", "vocab"), P("rows"), P("rows"), P("rows", None)),
        check_vma=False,
    )
```

```python
import functools
import math

import jax
import jax.numpy as jnp
from jax import lax
from jax.experimental import pallas as pl
from jax.experimental.pallas import tpu as pltpu
from jax.sharding import PartitionSpec as P

BEAMS = 8


soft_cap = 30.0
length_power = 0.6
norm_eps = 1e-06


def by_parent(values, parents):
    groups = values.reshape(-1, 1, BEAMS)
    hit = parents.reshape(-1, BEAMS, 1) == jnp.arange(BEAMS, dtype=jnp.int32)
    return jnp.sum(jnp.where(hit, groups, 0.0), axis=2).reshape(-1)


def plain(shards, hidden, norm_gain, embed_table, tokens, parents, prev_scores, lengths):
    shard_index = lax.axis_index("vocab")
    voc_rows = embed_table.shape[0]
    row_count, width = hidden.shape
    scale = math.sqrt(width)

    all_tokens = lax.all_gather(tokens, "rows", axis=0, tiled=False)
    groups = all_tokens.shape[0]
    piece = row_count // shards
    order = all_tokens.reshape(groups, shards, piece).transpose(1, 0, 2).reshape(-1)
    all_col = order - shard_index * voc_rows
    all_inside = (all_col >= 0) & (all_col < voc_rows)
    picked = jnp.take(embed_table, jnp.clip(all_col, 0, voc_rows - 1), axis=0)
    picked = jnp.where(all_inside[:, None], picked, jnp.zeros((), jnp.bfloat16))
    summed = lax.psum_scatter(picked, "vocab", scatter_dimension=0, tiled=True)

    states = hidden.astype(jnp.float32)
    meansq = jnp.mean(states * states, axis=-1, keepdims=True)
    normed = (states * lax.rsqrt(meansq + norm_eps) * norm_gain.astype(jnp.float32)).astype(
        jnp.bfloat16
    )
    feature_cols = lax.all_to_all(normed, "rows", split_axis=1, concat_axis=0, tiled=True)
    logits = lax.psum_scatter(
        lax.dot_general(
            feature_cols, embed_table, (((1,), (1,)), ((), ())), preferred_element_type=jnp.float32
        ).astype(jnp.bfloat16),
        "rows",
        scatter_dimension=0,
        tiled=True,
    ).astype(jnp.float32)

    quarter = lax.all_to_all(summed, "rows", split_axis=0, concat_axis=1, tiled=True)
    quarter = (quarter.astype(jnp.float32) * scale).astype(jnp.bfloat16)
    next_embed = lax.all_gather(quarter, "vocab", axis=0, tiled=True)

    local_col = tokens - shard_index * voc_rows
    inside = (local_col >= 0) & (local_col < voc_rows)
    clipped_col = jnp.clip(local_col, 0, voc_rows - 1)
    capped = soft_cap * jnp.tanh(logits / soft_cap)
    sum_exp = jnp.sum(jnp.exp(capped), axis=1)
    parent_rows = jnp.arange(row_count, dtype=jnp.int32) // BEAMS * BEAMS + parents
    chosen_local = jnp.where(inside, capped[parent_rows, clipped_col], 0.0)
    total_exp, chosen_logit = lax.psum((sum_exp, chosen_local), "vocab")
    lse = jnp.log(total_exp)
    log_probs = capped - lse[:, None]
    chosen_lp = chosen_logit - by_parent(lse, parents)
    penalty = jnp.power((5.0 + lengths.astype(jnp.float32)) / 6.0, length_power)
    normalized = (by_parent(prev_scores, parents) + chosen_lp) / penalty
    return (log_probs, chosen_lp, normalized, next_embed)


LINE = 4
QUARTERS = 4
TILES = 4
DEPTH = 512


def kernel(
    hidden_ref, gain_ref, table_ref, tokens_ref, parents_ref, scores_ref, cap_out, stat_out, emb_out,
    hid, table, nrm, far, aux, aux_in, tok_t, tok_p, acc, picked, from_z, from_x,
    quarters, emb, own, part_near, part_far, part_y, got_near, got_far, got_y, cap,
    sum_e, sum_c, stat_in, load_sem, out_sem, send_sem, recv_sem,
):
    v, r = lax.axis_index("vocab"), lax.axis_index("rows")
    z, x, y, c = v // 2, v % 2, r // 2, r % 2
    shards = 2 * LINE
    other_x = z * 2 + (1 - x)
    sib = y * 2 + (1 - c)
    far_same = (1 - y) * 2 + c
    far_sib = (1 - y) * 2 + (1 - c)
    voc_rows, depth = table.shape
    rows = hid.shape[0]
    piece = rows // shards
    width = voc_rows // TILES

    sites = []

    class Site:
        def __init__(self, src, dst, device):
            k = len(sites)
            sites.append(self)
            self.copy = pltpu.make_async_remote_copy(
                src_ref=src, dst_ref=dst, send_sem=send_sem.at[k], recv_sem=recv_sem.at[k],
                device_id=device, device_id_type=pl.DeviceIdType.MESH,
            )

        def start(self):
            self.copy.start()

        def sent(self):
            self.copy.wait_send()

        def arrived(self):
            self.copy.wait_recv()

    row_of = lax.broadcasted_iota(jnp.int32, (8, rows), 0)
    about = jnp.where(row_of == 0, tokens_ref[...].reshape(1, rows), parents_ref[...].reshape(1, rows))
    aux[...] = jnp.where(row_of < 2, about.astype(jnp.float32), scores_ref[...].reshape(1, rows))
    load_hidden = pltpu.make_async_copy(hidden_ref, hid, load_sem.at[0])
    load_table = pltpu.make_async_copy(table_ref, table, load_sem.at[1])
    load_hidden.start()
    load_table.start()

    barrier = pltpu.get_barrier_semaphore()
    for step in range(1, QUARTERS):
        pl.semaphore_signal(barrier, inc=1, device_id=(v, (r + step) % QUARTERS),
                            device_id_type=pl.DeviceIdType.MESH)
    for step in range(1, shards):
        pl.semaphore_signal(barrier, inc=1, device_id=((v + step) % shards, r),
                            device_id_type=pl.DeviceIdType.MESH)
    pl.semaphore_wait(barrier, QUARTERS + shards - 2)

    aux_sites = [Site(aux, aux_in.at[s], (v, (r + s) % QUARTERS)) for s in range(1, QUARTERS)]
    for site in aux_sites:
        site.start()

    load_hidden.wait()
    gain = gain_ref[...].astype(jnp.float32).reshape(1, QUARTERS * depth)

    def norm_step(i, _):
        at = pl.ds(pl.multiple_of(i * 16, 16), 16)
        states = hid[at, :].astype(jnp.float32)
        meansq = jnp.mean(states * states, axis=-1, keepdims=True)
        normed = (states * lax.rsqrt(meansq + norm_eps) * gain).astype(jnp.bfloat16)
        for q in range(QUARTERS):
            nrm[q, at, :] = normed[:, q * depth:(q + 1) * depth]
        return 0

    lax.fori_loop(0, rows // 16, norm_step, 0)
    hid_far_sib = Site(nrm.at[far_sib], far.at[0], (v, far_sib))
    hid_far_same = Site(nrm.at[far_same], far.at[1], (v, far_same))
    hid_sib = Site(nrm.at[sib], far.at[2], (v, sib))
    hid_sib.start()
    hid_far_sib.start()
    hid_far_same.start()

    def columns(block):
        return jnp.concatenate([block] * (128 // 8), axis=0).T

    tok_t[r] = columns(aux[...])
    for s, site in enumerate(aux_sites, 1):
        site.arrived()
        tok_t[(r + QUARTERS - s) % QUARTERS] = columns(aux_in[s])
    for p in range(shards):
        for q in range(QUARTERS):
            tok_p[p // 2, p % 2, q] = tok_t[q, p * piece:(p + 1) * piece, :]
    load_table.wait()

    base = (v * voc_rows).astype(jnp.float32)
    group = QUARTERS * piece

    def lookup(za, xa, zb, xb):
        tok = jnp.concatenate(
            [tok_p[za, xa].reshape(group, 128), tok_p[zb, xb].reshape(group, 128)], axis=0
        )[:, :1] - base

        def step(k, _):
            entry = lax.broadcasted_iota(jnp.int32, (2 * group, DEPTH), 1) + k * DEPTH
            hot = jnp.where(entry.astype(jnp.float32) == tok, 1.0, 0.0).astype(jnp.bfloat16)
            at = pl.ds(pl.multiple_of(k * DEPTH, DEPTH), DEPTH)
            acc[...] += jnp.dot(hot, table[at, :], preferred_element_type=jnp.float32)
            return 0

        acc[...] = jnp.zeros_like(acc)
        lax.fori_loop(0, voc_rows // DEPTH, step, 0)
        for half, (zz, xx) in enumerate(((za, xa), (zb, xb))):
            block = acc[half * group:(half + 1) * group, :].astype(jnp.bfloat16)
            picked[zz, xx] = block.reshape(QUARTERS, piece, depth)

    places = (LINE - 1 - z, (z + LINE // 2) % LINE, z + 1 - 2 * (z % 2), z)
    across = [Site(picked.at[j, 1 - x], from_x.at[k], (other_x, r)) for k, j in enumerate(places)]
    along = [Site(picked.at[j, x], from_z.at[k], (j * 2 + x, r)) for k, j in enumerate(places[:-1])]

    def add(dst, src):
        def one(i, _):
            dst[i] = dst[i] + src[i]
            return 0

        lax.fori_loop(0, QUARTERS, one, 0)

    def take(k):
        across[k].arrived()
        add(picked.at[places[k], x], from_x.at[k])
        if k < LINE - 1:
            along[k].start()

    for xx in (1 - x, x):
        for k in (0, 2):
            lookup(places[k], xx, places[k + 1], xx)
            if xx is not x:
                across[k].start()
                across[k + 1].start()

    def product(block, t):
        at = pl.ds(pl.multiple_of(t * width, width), width)
        return lax.dot_general(block, table[at, :], (((1,), (1,)), ((), ())),
                               preferred_element_type=jnp.float32)

    near_sites = [Site(part_near.at[t], got_near.at[t], (v, sib)) for t in range(TILES)]
    far_sites = [Site(part_far.at[t], got_far.at[t], (v, sib)) for t in range(TILES)]
    y_sites = [Site(part_y.at[t], got_y.at[t], (v, far_same)) for t in range(TILES)]

    take(0)

    def own_step(t, _):
        own[t] = product(nrm[r], t)
        return 0

    lax.fori_loop(0, TILES, own_step, 0)
    take(1)
    hid_sib.arrived()
    for t in range(TILES):
        part_near[t] = product(far[2], t).astype(jnp.bfloat16)
        near_sites[t].start()
    take(2)
    hid_far_sib.arrived()
    for t in range(TILES):
        part_far[t] = product(far[0], t).astype(jnp.bfloat16)
        far_sites[t].start()
    hid_far_same.arrived()
    for t in range(TILES):
        mine = product(far[1], t)
        far_sites[t].arrived()
        part_y[t] = (mine + got_far[t].astype(jnp.float32)).astype(jnp.bfloat16)
        if t < 1:
            y_sites[t].start()
    take(3)
    for k, site in enumerate(along):
        site.arrived()
        add(picked.at[z, x], from_z.at[k])

    quarter_sites = [
        Site(picked.at[z, x, (r + s) % QUARTERS], quarters.at[s], (v, (r + s) % QUARTERS))
        for s in range(1, QUARTERS)
    ]
    for site in quarter_sites:
        site.start()
    whole = emb.at[z, x]

    def place(q, block):
        for k in range(QUARTERS):
            @pl.when(q == k)
            def _(k=k):
                whole[:, k * depth:(k + 1) * depth] = block

    place(r, picked[z, x, r])
    for s, site in enumerate(quarter_sites, 1):
        site.arrived()
        place((r + QUARTERS - s) % QUARTERS, quarters[s])

    def piece_site(j, device):
        at = emb.at[j, x]
        return Site(at, at, (device, r))

    give = [piece_site(z, j * 2 + x) for j in places[:-1]]
    hand = [piece_site(j, other_x) for j in places]
    for k in (0, 1, 2):
        give[k].start()
    hand[LINE - 1].start()

    def gather_step(k):
        give[k].arrived()
        hand[k].start()

    for t in range(1, TILES):
        y_sites[t].start()

    sum_e[...] = jnp.zeros_like(sum_e)
    sum_c[...] = jnp.zeros_like(sum_c)
    some = 32
    out_copies = []

    def cap_tile(t):
        near_sites[t].arrived()
        y_sites[t].arrived()

        def cap_step(i, _):
            at = pl.ds(pl.multiple_of(i * some, some), some)
            logits = own[t, at, :] + got_near[t, at, :].astype(jnp.float32)
            logits = logits + got_y[t, at, :].astype(jnp.float32)
            capped = soft_cap * jnp.tanh(logits / soft_cap)
            cap[at, t * width:(t + 1) * width] = capped
            exps = jnp.exp(capped)
            about = tok_t[r, at, :]
            parent = about[:, 1:2].reshape(some // BEAMS, BEAMS, 1)
            beams = capped.reshape(some // BEAMS, BEAMS, width)
            chosen = jnp.zeros_like(beams)
            for b in range(BEAMS):
                chosen = jnp.where(parent == float(b), beams[:, b:b + 1, :], chosen)
            entry = lax.broadcasted_iota(jnp.int32, (some, width), 1) + t * width
            hit = entry.astype(jnp.float32) == about[:, 0:1] - base
            chosen = jnp.where(hit, chosen.reshape(some, width), 0.0)
            for k in range(0, width, 128):
                sum_e[at, :] += exps[:, k:k + 128]
                sum_c[at, :] += chosen[:, k:k + 128]
            return 0

        lax.fori_loop(0, rows // some, cap_step, 0)
        span = pl.ds(t * width, width)
        copy = pltpu.make_async_copy(cap.at[:, span], cap_out.at[:, span], out_sem.at[t])
        copy.start()
        out_copies.append(copy)

    cap_tile(0)
    gather_step(2)
    gather_step(0)
    for t in range(1, TILES):
        cap_tile(t)
    lane = lax.broadcasted_iota(jnp.int32, (rows, 128), 1)
    total_e = jnp.sum(sum_e[...], axis=1, keepdims=True)
    total_c = jnp.sum(sum_c[...], axis=1, keepdims=True)
    mine = tok_t[r]
    parent = mine[:, 1:2].reshape(rows // BEAMS, BEAMS, 1)

    def of_parent(column):
        beams = column.reshape(rows // BEAMS, BEAMS, 1)
        found = jnp.zeros_like(beams)
        for b in range(BEAMS):
            found = jnp.where(parent == float(b), beams[:, b:b + 1, :], found)
        return found.reshape(rows, 1)

    parent_e = of_parent(total_e)
    parent_score = of_parent(mine[:, 2:3])
    stat = jnp.where(lane == 0, total_e, jnp.where(lane == 1, total_c, jnp.where(lane == 2, parent_e, 0.0))).T[:8]
    scores = jnp.where(lane == 3, parent_score, 0.0).T[:8]
    stat_in[0] = stat
    stat_sites = [Site(stat_in.at[0], stat_in.at[s], ((v + s) % shards, r)) for s in range(1, shards)]
    for site in stat_sites:
        site.start()

    gather_step(1)
    for site in hand:
        site.arrived()
    emb_copy = pltpu.make_async_copy(emb, emb_out, out_sem.at[TILES])
    emb_copy.start()
    for s, site in enumerate(stat_sites, 1):
        site.arrived()
        stat = stat + stat_in[s]
    stat_out[...] = stat + scores
    for site in sites:
        site.sent()
    for copy in out_copies:
        copy.wait()
    emb_copy.wait()


def fused(hidden, norm_gain, embed_table, tokens, parents, prev_scores, lengths):
    shards = 2 * LINE
    voc_rows, depth = embed_table.shape
    rows, features = hidden.shape
    piece = rows // shards
    width = voc_rows // TILES
    half, full = jnp.bfloat16, jnp.float32
    anywhere, vmem = pl.BlockSpec(memory_space=pl.ANY), pl.BlockSpec(memory_space=pltpu.VMEM)
    stay = pl.BlockSpec(memory_space=pltpu.HBM)
    tiles = pltpu.VMEM((TILES, rows, width), half)
    line = pltpu.VMEM((LINE, 2, QUARTERS, piece, depth), half)
    capped, stat, raw = pl.pallas_call(
        kernel,
        out_shape=(
            jax.ShapeDtypeStruct((rows, voc_rows), full),
            jax.ShapeDtypeStruct((8, rows), full),
            jax.ShapeDtypeStruct((LINE, 2, piece, features), half),
        ),
        in_specs=[stay, vmem, stay, vmem, vmem, vmem],
        out_specs=(anywhere, vmem, anywhere),
        scratch_shapes=[
            pltpu.VMEM((rows, features), half),
            pltpu.VMEM((voc_rows, depth), half),
            pltpu.VMEM((QUARTERS, rows, depth), half),
            pltpu.VMEM((3, rows, depth), half),
            pltpu.VMEM((8, rows), full),
            pltpu.VMEM((QUARTERS, 8, rows), full),
            pltpu.VMEM((QUARTERS, rows, 128), full),
            pltpu.VMEM((LINE, 2, QUARTERS, piece, 128), full),
            pltpu.VMEM((2 * QUARTERS * piece, depth), full),
            line,
            pltpu.VMEM((LINE - 1, QUARTERS, piece, depth), half),
            pltpu.VMEM((LINE, QUARTERS, piece, depth), half),
            pltpu.VMEM((QUARTERS, piece, depth), half),
            pltpu.VMEM((LINE, 2, piece, features), half),
            pltpu.VMEM((TILES, rows, width), full),
            tiles, tiles, tiles, tiles, tiles, tiles,
            pltpu.VMEM((rows, voc_rows), full),
            pltpu.VMEM((rows, 128), full),
            pltpu.VMEM((rows, 128), full),
            pltpu.VMEM((shards, 8, rows), full),
            pltpu.SemaphoreType.DMA((2,)),
            pltpu.SemaphoreType.DMA((TILES + 1,)),
            pltpu.SemaphoreType.DMA((80,)),
            pltpu.SemaphoreType.DMA((80,)),
        ],
        compiler_params=pltpu.CompilerParams(
            collective_id=0, has_side_effects=True, vmem_limit_bytes=57 * 2**20
        ),
        cost_estimate=pl.CostEstimate(
            flops=8 * rows * QUARTERS // 2 * voc_rows * depth, bytes_accessed=12 * 2**20,
            transcendentals=2 * rows * voc_rows,
        ),
    )(hidden, norm_gain, embed_table, tokens, parents, prev_scores)
    lse = jnp.log(stat[0])
    log_probs = capped - lse[:, None]
    chosen_lp = stat[1] - jnp.log(stat[2])
    penalty = jnp.power((5.0 + lengths.astype(full)) / 6.0, length_power)
    normalized = (stat[3] + chosen_lp) / penalty
    next_embed = (raw.reshape(rows, features).astype(full) * math.sqrt(features)).astype(half)
    return (log_probs, chosen_lp, normalized, next_embed)


def solution(mesh):
    placed = (P("rows", None), P(), P("vocab", "rows"), P("rows"), P("rows"), P("rows"), P("rows"))
    shards = mesh.shape["vocab"]
    fits = shards == 2 * LINE and mesh.shape["rows"] == QUARTERS
    return jax.shard_map(
        fused if fits else functools.partial(plain, shards),
        mesh=mesh,
        in_specs=placed,
        out_specs=(P("rows", "vocab"), P("rows"), P("rows"), P("rows", None)),
        check_vma=False,
    )
```
